512 devices in a mesh: section: 2 (over core), batch: 8 (over z_hi, y), chan: 32 (over z_lo, x).
Axes of the slice: x: 4, y: 4, z: 16 (z_hi: 2, z_lo: 8; z = z_hi * 8 + z_lo), core: 2. Of those that a mesh axis runs over, the one named last changes fastest.
Arguments:
- activations: bfloat16 [2, 1, 64, 64, 1024], P('section', None, 'batch'), may hold values from -14 to 14
- kernel_a: bfloat16 [3, 3, 1024, 1024], P(None, None, None, 'chan'), may hold values from -0.0625 to 0.0625
- gain_a: float32 [1024], P('chan'), may hold values from 0.1 to 1.9
- bias_a: float32 [1024], P('chan'), may hold values from -0.5 to 0.5
- w_up: bfloat16 [1024, 4096], P(None, 'chan'), may hold values from -0.1875 to 0.1875
- gain_b: float32 [4096], P('chan'), may hold values from 0.1 to 1.9
- bias_b: float32 [4096], P('chan'), may hold values from -0.5 to 0.5
- w_down: bfloat16 [4096, 1024], P('chan'), may hold values from -0.09375 to 0.09375
- grad_out: bfloat16 [2, 1, 64, 64, 1024], P('section', None, 'batch', None, 'chan'), may hold values from -6 to 6
Outputs:
- block_output: bfloat16 [2, 1, 64, 64, 1024], P('section', None, 'batch', None, 'chan')
- grad_x: bfloat16 [2, 1, 64, 64, 1024], P('section', None, 'batch', None, 'chan')
- grad_kernel_a: float32 [3, 3, 1024, 1024], P(None, None, None, 'chan')
- grad_gain_a: float32 [1024], P('chan')
- grad_bias_a: float32 [1024], P('chan')
- grad_w_up: float32 [1024, 4096], P(None, 'chan')
- grad_gain_b: float32 [4096], P('chan')
- grad_bias_b: float32 [4096], P('chan')
- grad_w_down: float32 [4096, 1024], P('chan')
The draws below stay inside these ranges and needn't reach their ends.
All inputs are finite; a program needn't handle non-finite values.
Results may differ from the reference program's by a relative error of at most 0.034.
The reference program's roundings to bfloat16 on the way count: a program that leaves them out, or rounds other values in their place, can miss the bound.
Values may be sent and summed in bfloat16 or wider, within the bound.
No kernel may reach another device: no remote copies, remote signals or barrier semaphores. Data moves between devices by JAX's collectives and lax.ppermute only.
A program may use at most 64 MiB of HBM per device.

```python
import jax
import jax.numpy as jnp
from jax import lax

C = 1024
B = 4096
M = 1
WD = 64
MB = 2
NH = 64
N_CHAN = 32


def draw_activations(key, part):
    key_base, key_shift = jax.random.split(key, 2)
    row_frac = jnp.arange(NH, dtype=jnp.float32) / max(NH - 1, 1)
    row_scale = 0.5 * 3.0 ** row_frac
    shift = 0.3 * jax.random.normal(key_shift, (C,), jnp.float32)
    base = jnp.clip(jax.random.normal(key_base, (MB, M, NH, WD, C), jnp.float32), -6.0, 6.0)
    return (base * row_scale[:, None, None] + shift).astype(jnp.bfloat16)


def steps_of(key, extent, cuts, smallest, largest):
    def one(position, blocks):
        draws = jax.random.uniform(jax.random.fold_in(jax.random.fold_in(key, 6), position), (blocks,), jnp.float32, smallest / len(cuts), largest / len(cuts))
        return jnp.repeat(jnp.exp(draws), extent[position] // blocks).reshape((-1,) + (1,) * (len(extent) - position - 1))

    loudness = one(*cuts[0])
    for cut in cuts[1:]:
        loudness = loudness * one(*cut)
    return loudness


def scatter_about(key, extent, deviation, most, cuts=(), kind=jnp.bfloat16):
    result = jax.random.normal(key, extent, jnp.float32) * deviation
    if len(cuts) > 0:
        result = steps_of(key, extent, cuts, -0.22, 0.18) * result
    return jnp.clip(result, min=-most, max=most).astype(kind)


def setup_inputs(seed: int = 0) -> dict:
    key_list = jax.random.split(jax.random.key(seed), 10)
    return {
        "activations": draw_activations(jax.random.fold_in(key_list[9], 71), 0),
        "kernel_a": scatter_about(key_list[1], (3, 3, C, C), (9 * C) ** -0.5, 0.0625, ((3, 32),)),
        "gain_a": jnp.clip(1.0 + 0.18 * jax.random.normal(key_list[2], (C,), jnp.float32), 0.1, 1.9),
        "bias_a": jnp.clip(jax.random.uniform(key_list[3], (C,), jnp.float32, -0.5, 0.5) * steps_of(key_list[3], (C,), ((0, 32),), -0.4, 0.0), -0.5, 0.5),
        "w_up": scatter_about(key_list[4], (C, B), C ** -0.5, 0.1875, ((1, 32),)),
        "gain_b": jnp.clip(1.0 + 0.18 * jax.random.normal(key_list[5], (B,), jnp.float32), 0.1, 1.9),
        "bias_b": jnp.clip(jax.random.uniform(key_list[6], (B,), jnp.float32, -0.5, 0.5) * steps_of(key_list[6], (B,), ((0, 32),), -0.4, 0.0), -0.5, 0.5),
        "w_down": scatter_about(key_list[7], (B, C), B ** -0.5, 0.09375, ((0, 32),)),
        "grad_out": scatter_about(key_list[8], (MB, M, NH, WD, C), 1.0, 6.0, ((0, 2), (2, 8), (4, 32))),
    }


EPSILON = 1e-05

def rounded(value):
    return lax.optimization_barrier(value.astype(jnp.bfloat16)).astype(jnp.float32)

def conv_taps(padded, kernel, height, columns):
    summed = jnp.zeros((padded.shape[0] * height * columns, kernel.shape[3]), jnp.float32)
    for tap_row in range(3):
        for tap_col in range(3):
            window = padded[:, tap_row:tap_row + height, tap_col:tap_col + columns, :].reshape(-1, kernel.shape[2])
            summed = summed + jnp.dot(window, kernel[tap_row, tap_col], preferred_element_type=jnp.float32)
    return summed

def hidden_block(y_flat, g_flat, w_up, gain_b, bias_b, w_down, pixel_count):
    block = B // N_CHAN
    blocks = N_CHAN
    up_blocks = w_up.reshape(C, blocks, block).transpose(1, 0, 2)
    down_blocks = w_down.reshape(blocks, block, C)
    gain_blocks = gain_b.reshape(blocks, block)
    bias_blocks = bias_b.reshape(blocks, block)

    def step(carry, pieces):
        down_sum, back_sum = carry
        up_part, gain_part, bias_part, down_part = pieces
        hidden = jnp.dot(y_flat, up_part, preferred_element_type=jnp.float32)
        mean_b = lax.optimization_barrier(jnp.sum(hidden, 0)) / pixel_count
        var_b = lax.optimization_barrier(jnp.sum(hidden * hidden, 0)) / pixel_count - mean_b * mean_b
        scale_b = lax.rsqrt(var_b + EPSILON)
        norm_b = (hidden - mean_b) * scale_b
        pre_b = gain_part * norm_b + bias_part
        activated = jnp.maximum(pre_b, 0.0).astype(jnp.bfloat16)
        down_sum = down_sum + rounded(jnp.dot(activated, down_part, preferred_element_type=jnp.float32))
        back_hidden = jnp.dot(g_flat, down_part.T, preferred_element_type=jnp.float32)
        down_grad = jnp.dot(activated.T, g_flat, preferred_element_type=jnp.float32)
        masked = jnp.where(pre_b > 0, back_hidden, 0.0)
        first_sum = lax.optimization_barrier(jnp.sum(masked, 0))
        second_sum = lax.optimization_barrier(jnp.sum(masked * norm_b, 0))
        delta_u = (gain_part * scale_b * (masked - first_sum / pixel_count - norm_b * second_sum / pixel_count)).astype(jnp.bfloat16)
        up_grad = jnp.dot(y_flat.T, delta_u, preferred_element_type=jnp.float32)
        back_sum = back_sum + rounded(jnp.dot(delta_u, up_part.T, preferred_element_type=jnp.float32))
        return ((down_sum, back_sum), (up_grad, down_grad, first_sum, second_sum))
    zeros = jnp.zeros((y_flat.shape[0], C), jnp.float32)
    (down_sum, back_sum), stacked = lax.scan(step, (zeros, zeros), (up_blocks, gain_blocks, bias_blocks, down_blocks))
    up_grad = stacked[0].transpose(1, 0, 2).reshape(C, B)
    down_grad = stacked[1].reshape(B, C)
    return (down_sum, back_sum, up_grad, down_grad, stacked[2].reshape(B), stacked[3].reshape(B))

def reference(activations, kernel_a, gain_a, bias_a, w_up, gain_b, bias_b, w_down, grad_out):
    pixel_count = M * NH * WD
    block_c = C // N_CHAN
    outputs = []
    grads_x = []
    kernel_grad = jnp.zeros((3, 3, C, C), jnp.float32)
    gain_a_grad = jnp.zeros((C,), jnp.float32)
    bias_a_grad = jnp.zeros((C,), jnp.float32)
    up_total = jnp.zeros((C, B), jnp.float32)
    down_total = jnp.zeros((B, C), jnp.float32)
    gain_b_grad = jnp.zeros((B,), jnp.float32)
    bias_b_grad = jnp.zeros((B,), jnp.float32)
    kernel_blocks = kernel_a.reshape(3, 3, C, N_CHAN, block_c).transpose(3, 0, 1, 2, 4)
    for micro in range(MB):
        x_micro = activations[micro]
        padded = jnp.pad(x_micro, ((0, 0), (1, 1), (1, 1), (0, 0)))
        conv_a = conv_taps(padded, kernel_a, NH, WD)
        mean_a = lax.optimization_barrier(jnp.sum(conv_a, 0)) / pixel_count
        var_a = lax.optimization_barrier(jnp.sum(conv_a * conv_a, 0)) / pixel_count - mean_a * mean_a
        scale_a = lax.rsqrt(var_a + EPSILON)
        norm_a = (conv_a - mean_a) * scale_a
        pre_a = gain_a * norm_a + bias_a
        x_flat = x_micro.reshape(-1, C)
        y_flat = (x_flat.astype(jnp.float32) + jnp.maximum(pre_a, 0.0)).astype(jnp.bfloat16)
        g_flat = grad_out[micro].reshape(-1, C)
        down_sum, back_sum, up_grad, down_grad, first_b, second_b = hidden_block(y_flat, g_flat, w_up, gain_b, bias_b, w_down, pixel_count)
        outputs.append((y_flat.astype(jnp.float32) + down_sum).astype(jnp.bfloat16).reshape(M, NH, WD, C))
        up_total = up_total + up_grad
        down_total = down_total + down_grad
        gain_b_grad = gain_b_grad + second_b
        bias_b_grad = bias_b_grad + first_b
        grad_y = g_flat.astype(jnp.float32) + back_sum
        masked_a = jnp.where(pre_a > 0, grad_y, 0.0)
        first_a = lax.optimization_barrier(jnp.sum(masked_a, 0))
        second_a = lax.optimization_barrier(jnp.sum(masked_a * norm_a, 0))
        delta_a = (gain_a * scale_a * (masked_a - first_a / pixel_count - norm_a * second_a / pixel_count)).astype(jnp.bfloat16)
        gain_a_grad = gain_a_grad + second_a
        bias_a_grad = bias_a_grad + first_a
        tap_grads = []
        for tap_row in range(3):
            for tap_col in range(3):
                window = padded[:, tap_row:tap_row + NH, tap_col:tap_col + WD, :].reshape(-1, C)
                tap_grads.append(jnp.dot(window.T, delta_a, preferred_element_type=jnp.float32))
        kernel_grad = kernel_grad + jnp.stack(tap_grads).reshape(3, 3, C, C)
        delta_pad = jnp.pad(delta_a.reshape(M, NH, WD, C), ((0, 0), (1, 1), (1, 1), (0, 0)))
        delta_blocks = delta_pad.reshape(M, NH + 2, WD + 2, N_CHAN, block_c).transpose(3, 0, 1, 2, 4)

        def conv_block(total, pieces):
            kernel_part, delta_part = pieces
            part = jnp.zeros((M * NH * WD, C), jnp.float32)
            for tap_row in range(3):
                for tap_col in range(3):
                    window = delta_part[:, 2 - tap_row:2 - tap_row + NH, 2 - tap_col:2 - tap_col + WD, :].reshape(-1, block_c)
                    part = part + jnp.dot(window, kernel_part[tap_row, tap_col].T, preferred_element_type=jnp.float32)
            return (total + rounded(part), None)
        back_conv, _ = lax.scan(conv_block, jnp.zeros((M * NH * WD, C), jnp.float32), (kernel_blocks, delta_blocks))
        grads_x.append((grad_y + back_conv).astype(jnp.bfloat16).reshape(M, NH, WD, C))
    return (jnp.stack(outputs), jnp.stack(grads_x), kernel_grad, gain_a_grad, bias_a_grad, up_total, gain_b_grad, bias_b_grad, down_total)
```

```python
import jax
import jax.numpy as jnp
from jax import lax
from jax.sharding import PartitionSpec as P

EPSILON = 1e-05
F32 = jnp.float32
BF16 = jnp.bfloat16
NX = 4


def x_groups(n):
    return [[NX * z + i for i in range(NX)] for z in range(n // NX)]


def z_groups(n):
    return [[NX * z + i for z in range(n // NX)] for i in range(NX)]


def copies(value, n):
    return jnp.broadcast_to(value[None], (n,) + value.shape)


def gather_chan(own):
    n = lax.axis_size("chan")
    nz = n // NX
    line = lax.all_to_all(copies(own, nz), "chan", 0, 0, axis_index_groups=z_groups(n))
    line = line.reshape(nz * own.shape[0], own.shape[1])
    full = lax.all_to_all(copies(line, NX), "chan", 0, 0, axis_index_groups=x_groups(n))
    return full.reshape(n * own.shape[0], own.shape[1])


def scatter_chan(term):
    n = lax.axis_size("chan")
    nz = n // NX
    rows, cols = term.shape
    part = term.astype(BF16).reshape(NX, rows // NX, cols)
    part = lax.all_to_all(part, "chan", 0, 0, axis_index_groups=x_groups(n))
    part = jnp.sum(part.astype(F32), 0).astype(BF16).reshape(nz, rows // n, cols)
    part = lax.all_to_all(part, "chan", 0, 0, axis_index_groups=z_groups(n))
    return jnp.sum(part.astype(F32), 0)


def sum_batch(value):
    n = lax.axis_size("batch")
    return jnp.sum(lax.all_to_all(copies(value, n), "batch", 0, 0), 0)


def by_xz(array, n):
    block = array.shape[0] // n
    split = array.reshape(n // NX, NX, block, *array.shape[1:])
    return jnp.swapaxes(split, 0, 1).reshape(array.shape)


def by_zx(array, n):
    block = array.shape[0] // n
    split = array.reshape(NX, n // NX, block, *array.shape[1:])
    return jnp.swapaxes(split, 0, 1).reshape(array.shape)


def other_section(value):
    return lax.ppermute(value, "section", [(0, 1), (1, 0)])


def sum_grads(grad):
    rows, cols = grad.shape
    half = rows // 2
    ny = 4
    nb = lax.axis_size("batch")
    me = lax.axis_index("section")
    mine = lax.dynamic_slice_in_dim(grad, me * half, half, 0)
    theirs = lax.dynamic_slice_in_dim(grad, (1 - me) * half, half, 0)
    part = (mine.astype(F32) + other_section(theirs).astype(F32)).astype(BF16)
    y_groups = [[ny * z + i for i in range(ny)] for z in range(nb // ny)]
    part = part.reshape(ny, half // ny, cols)
    part = lax.all_to_all(part, "batch", 0, 0, axis_index_groups=y_groups)
    part = jnp.sum(part.astype(F32), 0).astype(BF16)
    across = lax.ppermute(part, "batch", [(i, (i + ny) % nb) for i in range(nb)])
    part = (part.astype(F32) + across.astype(F32)).astype(BF16)
    part = lax.all_to_all(copies(part, ny), "batch", 0, 0, axis_index_groups=y_groups)
    part = part.reshape(half, cols)
    rest = other_section(part)
    first = jnp.where(me == 0, part, rest)
    second = jnp.where(me == 0, rest, part)
    return jnp.concatenate([first, second], 0)


def halo(array, axis):
    n = lax.axis_size("batch")
    up = [(i, i + 1) for i in range(n - 1)]
    down = [(j, i) for i, j in up]
    length = array.shape[axis]
    before = lax.ppermute(lax.slice_in_dim(array, length - 1, length, axis=axis), "batch", up)
    after = lax.ppermute(lax.slice_in_dim(array, 0, 1, axis=axis), "batch", down)
    return jnp.concatenate([before, array, after], axis=axis)


def body(activations, kernel_a, gain_a, bias_a, w_up, gain_b, bias_b, w_down, grad_out):
    rows, columns, channels = activations.shape[2:]
    width = kernel_a.shape[3]
    n_chan = lax.axis_size("chan")
    local = rows * columns
    pixel_count = local * lax.axis_size("batch")
    gain_a, bias_a = gain_a[:, None], bias_a[:, None]
    gain_b, bias_b = gain_b[:, None], bias_b[:, None]

    x_own = activations[0, 0]
    taps = kernel_a.transpose(0, 1, 3, 2).reshape(9 * width, channels)
    x_halo = halo(x_own, 0).reshape((rows + 2) * columns, channels)
    cotan_own = grad_out[0, 0].transpose(2, 0, 1).reshape(width, local)
    up_rows = by_xz(w_up, n_chan)
    down_rows = by_xz(w_down.T, n_chan)

    partial = lax.dot_general(taps, x_halo, (((1,), (1,)), ((), ())), preferred_element_type=F32)
    partial = partial.reshape(3, 3, width, rows + 2, columns)
    conv_a = jnp.zeros((width, rows, columns), F32)
    for tap_row in range(3):
        for tap_col in range(3):
            piece = partial[tap_row, tap_col, :, tap_row : tap_row + rows]
            if tap_col == 0:
                piece = jnp.pad(piece[:, :, :-1], ((0, 0), (0, 0), (1, 0)))
            if tap_col == 2:
                piece = jnp.pad(piece[:, :, 1:], ((0, 0), (0, 0), (0, 1)))
            conv_a = conv_a + piece
    conv_a = conv_a.reshape(width, local)
    sums_a = sum_batch(jnp.stack([jnp.sum(conv_a, 1), jnp.sum(conv_a * conv_a, 1)]))
    mean_a = sums_a[0][:, None] / pixel_count
    var_a = sums_a[1][:, None] / pixel_count - mean_a * mean_a
    scale_a = lax.rsqrt(var_a + EPSILON)
    norm_a = (conv_a - mean_a) * scale_a
    pre_a = gain_a * norm_a + bias_a
    source_own = lax.dynamic_slice_in_dim(
        x_own.reshape(local, channels), lax.axis_index("chan") * width, width, 1
    ).T
    stream_own = (source_own.astype(F32) + jnp.maximum(pre_a, 0.0)).astype(BF16)

    cotan_full = gather_chan(cotan_own)
    stream_full = gather_chan(stream_own)
    hidden = lax.dot_general(
        up_rows, stream_full, (((0,), (0,)), ((), ())), preferred_element_type=F32
    )
    sums_b = sum_batch(jnp.stack([jnp.sum(hidden, 1), jnp.sum(hidden * hidden, 1)]))
    mean_b = sums_b[0][:, None] / pixel_count
    var_b = sums_b[1][:, None] / pixel_count - mean_b * mean_b
    scale_b = lax.rsqrt(var_b + EPSILON)
    norm_b = (hidden - mean_b) * scale_b
    pre_b = gain_b * norm_b + bias_b
    activated = jnp.maximum(pre_b, 0.0).astype(BF16)

    back_hidden = lax.dot_general(
        down_rows, cotan_full, (((0,), (0,)), ((), ())), preferred_element_type=F32
    )
    masked_b = jnp.where(pre_b > 0, back_hidden, 0.0)
    back_b = sum_batch(jnp.stack([jnp.sum(masked_b, 1), jnp.sum(masked_b * norm_b, 1)]))
    delta_u = (
        gain_b
        * scale_b
        * (
            masked_b
            - back_b[0][:, None] / pixel_count
            - norm_b * back_b[1][:, None] / pixel_count
        )
    ).astype(BF16)
    up_term = jnp.dot(up_rows, delta_u, preferred_element_type=F32)
    grad_y = cotan_own.astype(F32) + scatter_chan(up_term)

    masked_a = jnp.where(pre_a > 0, grad_y, 0.0)
    back_a = sum_batch(jnp.stack([jnp.sum(masked_a, 1), jnp.sum(masked_a * norm_a, 1)]))
    delta_a = (
        gain_a
        * scale_a
        * (
            masked_a
            - back_a[0][:, None] / pixel_count
            - norm_a * back_a[1][:, None] / pixel_count
        )
    ).astype(BF16)
    delta_halo = halo(delta_a.reshape(width, rows, columns), 1)
    delta_pad = jnp.pad(delta_halo, ((0, 0), (0, 0), (1, 1)))
    windows = jnp.stack(
        [
            delta_pad[:, 2 - tap_row : 2 - tap_row + rows, 2 - tap_col : 2 - tap_col + columns]
            for tap_row in range(3)
            for tap_col in range(3)
        ]
    ).reshape(9 * width, local)
    back_conv = lax.dot_general(
        taps, windows, (((0,), (0,)), ((), ())), preferred_element_type=F32
    )
    conv_back = scatter_chan(by_xz(back_conv.astype(BF16), n_chan))
    grad_x = (grad_y + conv_back).astype(BF16)

    down_term = jnp.dot(down_rows, activated, preferred_element_type=F32)
    out_own = (stream_own.astype(F32) + scatter_chan(down_term)).astype(BF16)

    up_grad = lax.dot_general(
        stream_full, delta_u, (((1,), (1,)), ((), ())), preferred_element_type=F32
    )
    down_grad = lax.dot_general(
        cotan_full, activated, (((1,), (1,)), ((), ())), preferred_element_type=F32
    )
    kernel_grad = jnp.dot(windows, x_own.reshape(local, channels), preferred_element_type=F32)
    units = up_grad.shape[1]
    kernel_rows = kernel_grad.reshape(-1, units)
    grads = jnp.concatenate(
        [up_grad.astype(BF16), down_grad.astype(BF16), kernel_rows.astype(BF16)], 0
    )
    grads = sum_grads(grads)
    up_total = by_zx(grads[:channels].astype(F32), n_chan)
    down_total = by_zx(grads[channels : 2 * channels].astype(F32), n_chan).T
    kernel_total = grads[2 * channels :].astype(F32).reshape(3, 3, width, channels)
    kernel_total = kernel_total.transpose(0, 1, 3, 2)
    vectors = jnp.concatenate([back_a, back_b], 1)
    vectors = vectors + other_section(vectors)

    def placed(own):
        return own.reshape(width, rows, columns).transpose(1, 2, 0)[None, None]

    return (
        placed(out_own),
        placed(grad_x),
        kernel_total,
        vectors[1, :width],
        vectors[0, :width],
        up_total,
        vectors[1, width:],
        vectors[0, width:],
        down_total,
    )


def solution(mesh):
    placed = (
        P("section", None, "batch", None, None),
        P(None, None, None, "chan"),
        P("chan"),
        P("chan"),
        P(None, "chan"),
        P("chan"),
        P("chan"),
        P("chan", None),
        P("section", None, "batch", None, "chan"),
    )
    return jax.shard_map(
        body,
        mesh=mesh,
        in_specs=placed,
        out_specs=(
            P("section", None, "batch", None, "chan"),
            P("section", None, "batch", None, "chan"),
            P(None, None, None, "chan"),
            P("chan"),
            P("chan"),
            P(None, "chan"),
            P("chan"),
            P("chan"),
            P("chan", None),
        ),
        check_vma=False,
    )
```

```python
import functools

import jax
import jax.numpy as jnp
from jax import lax
from jax.experimental import pallas as pl
from jax.experimental.pallas import tpu as pltpu
from jax.sharding import PartitionSpec as P

EPSILON = 1e-05
F32 = jnp.float32
BF16 = jnp.bfloat16
NX = 4
NY = 4
LANES = 128
VMEM_LIMIT = 8 << 20
NT = (((1,), (1,)), ((), ()))
TN = (((0,), (0,)), ((), ()))


def x_groups(n):
    return [[NX * z + i for i in range(NX)] for z in range(n // NX)]


def z_groups(n):
    return [[NX * z + i for z in range(n // NX)] for i in range(NX)]


def y_groups(n):
    return [[NY * z + i for i in range(NY)] for z in range(n // NY)]


def along_x(parts):
    n = lax.axis_size("chan")
    return lax.all_to_all(parts, "chan", 0, 0, axis_index_groups=x_groups(n))


def along_z(parts):
    n = lax.axis_size("chan")
    return lax.all_to_all(parts, "chan", 0, 0, axis_index_groups=z_groups(n))


def along_y(parts):
    n = lax.axis_size("batch")
    return lax.all_to_all(parts, "batch", 0, 0, axis_index_groups=y_groups(n))


def along_batch(parts):
    return lax.all_to_all(parts, "batch", 0, 0)


def copies(value, n):
    return jnp.broadcast_to(value[None], (n,) + value.shape)


def by_xz(array, n):
    block = array.shape[0] // n
    split = array.reshape(n // NX, NX, block, *array.shape[1:])
    return jnp.swapaxes(split, 0, 1).reshape(array.shape)


def after(value, *others):
    return lax.optimization_barrier((value, *others))[0]


def partner(value, axis, step):
    n = lax.axis_size(axis)
    return lax.ppermute(value, axis, [(i, i ^ step) for i in range(n)])


def dot(a, b, dims=None):
    if dims is None:
        return jnp.dot(a, b, preferred_element_type=F32)
    return lax.dot_general(a, b, dims, preferred_element_type=F32)


def call(kernel, outs, arrays, scratch=()):
    vmem = pl.BlockSpec(memory_space=pltpu.VMEM)
    return pl.pallas_call(
        kernel,
        out_shape=tuple(jax.ShapeDtypeStruct(shape, dtype) for shape, dtype in outs),
        in_specs=[vmem] * len(arrays),
        out_specs=(vmem,) * len(outs),
        scratch_shapes=list(scratch),
        compiler_params=pltpu.CompilerParams(vmem_limit_bytes=VMEM_LIMIT),
    )(*arrays)


def lane_of(lanes):
    return lax.broadcasted_iota(jnp.int32, (1, lanes), 1)


def column_tile(first, second, start):
    lane = lane_of(LANES)
    return jnp.where(lane == start, first, jnp.where(lane == start + 1, second, 0.0))


def write_edges(out_ref, value, first, second, columns, me):
    local = value.shape[1]
    lane = lane_of(LANES)
    sums = column_tile(first, second, columns)
    low = jnp.where(lane < columns, value[:, :LANES], sums)
    last = pltpu.roll(value[:, local - LANES :], columns, 1)
    high = jnp.where(lane < columns, last, sums)
    for peer in range(out_ref.shape[0]):
        out_ref[peer] = jnp.where(me > peer, low, high)


def read_edges(in_ref, columns, me):
    count = in_ref.shape[0]
    total = in_ref[0]
    for peer in range(1, count):
        total = total + in_ref[peer]
    beyond = in_ref[jnp.minimum(me + 1, count - 1)]
    before = pltpu.roll(in_ref[jnp.maximum(me - 1, 0)], columns, 1)
    edge = jnp.where(lane_of(LANES) < columns, beyond, before)
    return edge, total[:, columns : columns + 1], total[:, columns + 1 : columns + 2]


def write_rows(out_ref, first, second):
    rows = column_tile(first, second, 0).T[:8]
    for peer in range(out_ref.shape[0]):
        out_ref[peer] = rows


def read_rows(in_ref):
    total = in_ref[0]
    for peer in range(1, in_ref.shape[0]):
        total = total + in_ref[peer]
    square = jnp.concatenate([total, jnp.zeros((LANES - 8, LANES), F32)], 0).T
    return total, square[:, 0:1], square[:, 1:2]


def shifted(value, offset, local):
    if offset != 0:
        value = pltpu.roll(value, (-offset) % value.shape[1], 1)
    return value[:, :local]


def conv_kernel(columns, x_ref, edge_ref, taps_ref, conv_ref, own_ref, pay_ref, part_ref):
    width, local = conv_ref.shape
    channels = x_ref.shape[1]
    part_ref[:, :local] = dot(taps_ref[...], x_ref[...], NT)
    part_ref[:, local:] = dot(taps_ref[...], edge_ref[...], NT)
    row = lax.broadcasted_iota(jnp.int32, (width, channels), 0) + lax.axis_index("chan") * width
    col = lax.broadcasted_iota(jnp.int32, (width, channels), 1)
    own_ref[...] = dot(jnp.where(row == col, 1.0, 0.0).astype(BF16), x_ref[...], NT)
    column = lax.rem(lane_of(local), columns)
    conv = jnp.zeros((width, local), F32)
    for tap in range(9):
        tap_row, tap_col = divmod(tap, 3)
        offset = (tap_row - 1) * columns + tap_col - 1
        piece = shifted(part_ref[tap * width : (tap + 1) * width, :], offset, local)
        if tap_col == 0:
            piece = jnp.where(column > 0, piece, 0.0)
        if tap_col == 2:
            piece = jnp.where(column < columns - 1, piece, 0.0)
        conv = conv + piece
    conv_ref[...] = conv
    first = jnp.sum(conv, 1, keepdims=True)
    second = jnp.sum(conv * conv, 1, keepdims=True)
    write_edges(pay_ref, conv, first, second, columns, lax.axis_index("batch"))


def stream_kernel(
    columns, pixels, conv_ref, own_ref, recv_ref, gain_ref, bias_ref, out_ref, norm_ref, fact_ref
):
    local = conv_ref.shape[1]
    edge, first, second = read_edges(recv_ref, columns, lax.axis_index("batch"))
    mean = first / pixels
    scale = lax.rsqrt(second / pixels - mean * mean + EPSILON)
    norm = (conv_ref[...] - mean) * scale
    norm_ref[:, :local] = norm
    norm_ref[:, local:] = (edge - mean) * scale
    pre = gain_ref[...] * norm + bias_ref[...]
    stream = (own_ref[...] + jnp.maximum(pre, 0.0)).astype(BF16)
    for peer in range(out_ref.shape[0]):
        out_ref[peer] = stream
    fact_ref[...] = jnp.broadcast_to(gain_ref[...] * scale, fact_ref.shape)


def hidden_kernel(full_ref, up_ref, hidden_ref, pay_ref):
    depth = full_ref.shape[1]
    hidden = jnp.zeros(hidden_ref.shape, F32)
    for i in range(NX):
        hidden = hidden + dot(up_ref[:, i * depth : (i + 1) * depth], full_ref[i])
    hidden_ref[...] = hidden
    write_rows(
        pay_ref,
        jnp.sum(hidden, 1, keepdims=True),
        jnp.sum(hidden * hidden, 1, keepdims=True),
    )


def active_kernel(
    pixels, hidden_ref, cotan_ref, recv_ref, gain_ref, bias_ref, cols_ref, rows_ref,
    act_ref, norm_ref, masked_ref, pay_ref, fact_ref, term_ref,
):
    _, first, second = read_rows(recv_ref)
    mean = first / pixels
    scale = lax.rsqrt(second / pixels - mean * mean + EPSILON)
    norm = (hidden_ref[...] - mean) * scale
    pre = gain_ref[...] * norm + bias_ref[...]
    act = jnp.maximum(pre, 0.0).astype(BF16)
    act_ref[...] = act
    masked = jnp.where(pre > 0, dot(cols_ref[...], cotan_ref[...]), 0.0)
    norm_ref[...] = norm
    masked_ref[...] = masked
    fact_ref[...] = jnp.broadcast_to(gain_ref[...] * scale, fact_ref.shape)
    write_rows(
        pay_ref,
        jnp.sum(masked, 1, keepdims=True),
        jnp.sum(masked * norm, 1, keepdims=True),
    )
    depth = term_ref.shape[0] // NX
    for i in range(NX):
        part = slice(i * depth, (i + 1) * depth)
        term_ref[part] = dot(rows_ref[part], act).astype(BF16)


def term_kernel(
    pixels, masked_ref, norm_ref, recv_ref, fact_ref, up_ref, delta_ref, term_ref, sums_ref
):
    total, first, second = read_rows(recv_ref)
    sums_ref[...] = total
    delta = fact_ref[:, 0:1] * (
        masked_ref[...] - first / pixels - norm_ref[...] * second / pixels
    )
    delta = delta.astype(BF16)
    delta_ref[...] = delta
    depth = term_ref.shape[1]
    for i in range(NX):
        part = slice(i * depth, (i + 1) * depth)
        term_ref[i] = dot(up_ref[part], delta).astype(BF16)


def weight_kernel(full_ref, cotan_ref, delta_ref, act_ref, grad_ref):
    depth = full_ref.shape[1]
    for i in range(NX):
        grad_ref[i] = dot(full_ref[i], delta_ref[...], NT).astype(BF16)
        cotan = cotan_ref[i * depth : (i + 1) * depth]
        grad_ref[NX + i] = dot(cotan, act_ref[...], NT).astype(BF16)


def sum_kernel(recv_ref, *refs):
    out_ref = refs[-1]
    rows = recv_ref.shape[1] // out_ref.shape[0]
    for z in range(out_ref.shape[0]):
        part = slice(z * rows, (z + 1) * rows)
        total = recv_ref[0, part].astype(F32)
        for i in range(1, NX):
            total = total + recv_ref[i, part].astype(F32)
        out_ref[z, :rows] = total.astype(BF16)
        for k, ref in enumerate(refs[:-1]):
            out_ref[z, (k + 1) * rows : (k + 2) * rows] = ref[part]


def grad_kernel(
    columns, recv_ref, cotan_ref, norm_ref, gain_ref, bias_ref, grad_ref, masked_ref, pay_ref
):
    width, local = grad_ref.shape
    total = recv_ref[0].astype(F32)
    for z in range(1, recv_ref.shape[0]):
        total = total + recv_ref[z].astype(F32)
    grad = cotan_ref[...].astype(F32) + total
    grad_ref[...] = grad
    norm = norm_ref[:, :local]
    masked = jnp.where(gain_ref[...] * norm + bias_ref[...] > 0, grad, 0.0)
    masked_ref[...] = masked
    first = jnp.sum(masked, 1, keepdims=True)
    second = jnp.sum(masked * norm, 1, keepdims=True)
    write_edges(pay_ref, masked, first, second, columns, lax.axis_index("batch"))


def back_kernel(
    columns, pixels, masked_ref, recv_ref, norm_ref, fact_ref, taps_ref, x_ref, weight_ref,
    term_ref, mine_ref, theirs_ref, sums_ref, win_ref,
):
    width, local = masked_ref.shape
    me = lax.axis_index("batch")
    edge, first, second = read_edges(recv_ref, columns, me)
    sums_ref[...] = column_tile(first, second, 0)
    masked = jnp.concatenate([masked_ref[...], edge], 1)
    delta = fact_ref[:, 0:1] * (masked - first / pixels - norm_ref[...] * second / pixels)
    lane = lane_of(local + LANES)
    beyond = (lane >= local) & (lane < local + columns)
    before = lane >= local + columns
    high = jnp.where(me == recv_ref.shape[0] - 1, 1, 0)
    low = jnp.where(me == 0, 1, 0)
    outside = jnp.where(beyond, high, jnp.where(before, low, 0))
    delta = jnp.where(outside > 0, 0.0, delta).astype(BF16).astype(F32)
    column = lax.rem(lane_of(local), columns)
    for tap in range(9):
        tap_row, tap_col = divmod(tap, 3)
        offset = (1 - tap_row) * columns + 1 - tap_col
        piece = shifted(delta, offset, local)
        if tap_col == 0:
            piece = jnp.where(column < columns - 1, piece, 0.0)
        if tap_col == 2:
            piece = jnp.where(column > 0, piece, 0.0)
        win_ref[tap * width : (tap + 1) * width, :] = piece.astype(BF16)
    depth = term_ref.shape[1]
    step = NX * width
    for z in range(depth // width):
        block = dot(taps_ref[:, z * step : (z + 1) * step], win_ref[...], TN).astype(BF16)
        for i in range(NX):
            term_ref[i, z * width : (z + 1) * width, :] = block[i * width : (i + 1) * width]
    rows = win_ref.shape[0]
    for ref, half in ((mine_ref, lax.axis_index("section")), (theirs_ref, 1 - lax.axis_index("section"))):
        for j in range(NY):
            chunk = half * NY + j
            start = pl.multiple_of(chunk * LANES, LANES)
            ref[j, :rows] = dot(win_ref[...], x_ref[:, pl.ds(start, LANES)]).astype(BF16)
            ref[j, rows:] = weight_ref[chunk]


def finish_kernel(recv_ref, grad_ref, stream_ref, grad_x_ref, out_ref):
    width = grad_ref.shape[0]
    total = recv_ref[0].astype(F32)
    for z in range(1, recv_ref.shape[0]):
        total = total + recv_ref[z].astype(F32)
    grad_x_ref[...] = (grad_ref[...] + total[:width]).astype(BF16)
    out_ref[...] = (stream_ref[0].astype(F32) + total[width:]).astype(BF16)


def spread_kernel(line_ref, rest_ref, taps_ref, up_ref, down_ref, hold_ref):
    rows = taps_ref.shape[0]
    width = rows // 9
    mine = lax.axis_index("section") == 0
    for chunk in range(2 * NY):
        j = chunk % NY
        a, b = line_ref[j], rest_ref[j]
        if chunk < NY:
            part = jnp.where(mine, a.astype(F32), b.astype(F32))
        else:
            part = jnp.where(mine, b.astype(F32), a.astype(F32))
        taps_ref[:, chunk * LANES : (chunk + 1) * LANES] = part[:rows]
        target = up_ref if chunk < NX else hold_ref
        for z in range((part.shape[0] - rows) // width):
            at = (z * NX + chunk % NX) * width
            target[at : at + width] = part[rows + z * width : rows + (z + 1) * width]
    for block in range(hold_ref.shape[0] // LANES):
        part = slice(block * LANES, (block + 1) * LANES)
        down_ref[:, part] = hold_ref[part].T


def body(activations, kernel_a, gain_a, bias_a, w_up, gain_b, bias_b, w_down, grad_out):
    rows, columns, channels = activations.shape[2:]
    width = kernel_a.shape[3]
    units = w_up.shape[1]
    n_chan = lax.axis_size("chan")
    n_batch = lax.axis_size("batch")
    nz = n_chan // NX
    local = rows * columns
    pixels = local * n_batch
    gain_a, bias_a = gain_a[:, None], bias_a[:, None]
    gain_b, bias_b = gain_b[:, None], bias_b[:, None]

    x_rows = activations.reshape(local, channels)
    taps = kernel_a.transpose(0, 1, 3, 2).reshape(9 * width, channels)
    cotan_own = grad_out[0, 0].transpose(2, 0, 1).reshape(width, local)
    cotan_line = along_z(copies(cotan_own, nz)).reshape(nz * width, local)
    cotan_full = lax.all_gather(
        cotan_line, "chan", axis_index_groups=x_groups(n_chan), tiled=True
    )
    up = [(i, i + 1) for i in range(n_batch - 1)]
    down = [(j, i) for i, j in up]
    before = lax.ppermute(x_rows[local - columns :], "batch", up)
    beyond = lax.ppermute(x_rows[:columns], "batch", down)
    edge = jnp.concatenate([beyond, before], 0)
    up_rows = by_xz(w_up, n_chan)
    down_rows = by_xz(w_down.T, n_chan)
    up_cols, down_cols = up_rows.T, down_rows.T

    conv_a, source, pay = call(
        functools.partial(conv_kernel, columns),
        [((width, local), F32), ((width, local), F32), ((n_batch, width, LANES), F32)],
        (x_rows, edge, taps),
        [pltpu.VMEM((9 * width, local + 2 * columns), F32)],
    )
    recv = along_batch(after(pay, cotan_line, up_cols, down_cols))
    stream, norm_a, fact_a = call(
        functools.partial(stream_kernel, columns, pixels),
        [
            ((nz, width, local), BF16),
            ((width, local + LANES), F32),
            ((width, LANES), F32),
        ],
        (conv_a, source, recv, gain_a, bias_a),
    )
    stream_line = along_z(stream)
    depth = nz * width
    full = along_x(copies(stream_line.reshape(depth, local), NX))
    hidden, pay = call(
        hidden_kernel,
        [((units, local), F32), ((n_batch, 8, LANES), F32)],
        (full, up_cols),
    )
    act, norm_b, masked_b, pay, fact_b, down_term = call(
        functools.partial(active_kernel, pixels),
        [
            ((units, local), BF16),
            ((units, local), F32),
            ((units, local), F32),
            ((n_batch, 8, LANES), F32),
            ((units, LANES), F32),
            ((channels, local), BF16),
        ],
        (hidden, cotan_full, along_batch(pay), gain_b, bias_b, down_cols, down_rows),
    )
    down_part = lax.psum_scatter(
        down_term, "chan", axis_index_groups=x_groups(n_chan), tiled=True
    )
    delta_u, term, sums_b = call(
        functools.partial(term_kernel, pixels),
        [((units, local), BF16), ((NX, depth, local), BF16), ((8, LANES), F32)],
        (masked_b, norm_b, along_batch(pay), fact_b, up_rows),
    )
    (weight_grad,) = call(
        weight_kernel, [((2 * NX, depth, units), BF16)], (full, cotan_full, delta_u, act)
    )
    (part,) = call(
        sum_kernel, [((nz, width, local), BF16)], (along_x(term),)
    )
    part = after(part, weight_grad, down_part)
    grad_y, masked_a, pay = call(
        functools.partial(grad_kernel, columns),
        [
            ((width, local), F32),
            ((width, local), F32),
            ((n_batch, width, LANES), F32),
        ],
        (along_z(part), cotan_own, norm_a, gain_a, bias_a),
    )
    taps_rows = 9 * width
    chunk_rows = taps_rows + depth
    term, mine, theirs, sums_a = call(
        functools.partial(back_kernel, columns, pixels),
        [
            ((NX, depth, local), BF16),
            ((NY, chunk_rows, LANES), BF16),
            ((NY, chunk_rows, LANES), BF16),
            ((width, LANES), F32),
        ],
        (masked_a, along_batch(pay), norm_a, fact_a, taps, x_rows, weight_grad),
        [pltpu.VMEM((taps_rows, local), BF16)],
    )
    recv = along_x(term)
    theirs = partner(theirs, "section", 1)
    vectors = jnp.concatenate([sums_a[:, :2].T, sums_b[:2]], 1)
    vectors = vectors + partner(vectors, "section", 1)
    half = (mine.astype(F32) + theirs.astype(F32)).astype(BF16)
    recv = after(recv, half, vectors)
    half = along_y(after(half, recv))
    half = jnp.sum(half.astype(F32), 0).astype(BF16)
    across = partner(half, "batch", NY)
    (part,) = call(sum_kernel, [((nz, 2 * width, local), BF16)], (recv, down_part))
    recv = along_z(after(part, half))
    grad_x, out_own = call(
        finish_kernel,
        [((width, local), BF16), ((width, local), BF16)],
        (recv, grad_y, stream),
    )
    half = (half.astype(F32) + across.astype(F32)).astype(BF16)
    line = along_y(copies(after(half, recv), NY))
    rest = partner(line, "section", 1)
    kernel_total, up_total, down_total = call(
        spread_kernel,
        [((taps_rows, channels), F32), ((channels, units), F32), ((units, channels), F32)],
        (line, rest),
        [pltpu.VMEM((channels, units), F32)],
    )
    kernel_total = kernel_total.reshape(3, 3, width, channels).transpose(0, 1, 3, 2)

    def placed(own):
        return own.reshape(width, rows, columns).transpose(1, 2, 0)[None, None]

    return (
        placed(out_own),
        placed(grad_x),
        kernel_total,
        vectors[1, :width],
        vectors[0, :width],
        up_total,
        vectors[1, width:],
        vectors[0, width:],
        down_total,
    )


def solution(mesh):
    placed = (
        P("section", None, "batch", None, None),
        P(None, None, None, "chan"),
        P("chan"),
        P("chan"),
        P(None, "chan"),
        P("chan"),
        P("chan"),
        P("chan", None),
        P("section", None, "batch", None, "chan"),
    )
    return jax.shard_map(
        body,
        mesh=mesh,
        in_specs=placed,
        out_specs=(
            P("section", None, "batch", None, "chan"),
            P("section", None, "batch", None, "chan"),
            P(None, None, None, "chan"),
            P("chan"),
            P("chan"),
            P(None, "chan"),
            P("chan"),
            P("chan"),
            P("chan", None),
        ),
        check_vma=False,
    )
```

```python
import functools

import jax
import jax.numpy as jnp
from jax import lax
from jax.experimental import pallas as pl
from jax.experimental.pallas import tpu as pltpu
from jax.sharding import PartitionSpec as P

EPSILON = 1e-05
F32 = jnp.float32
BF16 = jnp.bfloat16
NX = 4
NY = 4
LANES = 128
VMEM_LIMIT = 12 << 20
FAR_LIMIT = 56 << 20
NT = (((1,), (1,)), ((), ()))
TN = (((0,), (0,)), ((), ()))


def x_groups(n):
    return [[NX * z + i for i in range(NX)] for z in range(n // NX)]


def z_groups(n):
    return [[NX * z + i for z in range(n // NX)] for i in range(NX)]


def y_groups(n):
    return [[NY * z + i for i in range(NY)] for z in range(n // NY)]


def along_x(parts):
    n = lax.axis_size("chan")
    return lax.all_to_all(parts, "chan", 0, 0, axis_index_groups=x_groups(n))


def along_z(parts):
    n = lax.axis_size("chan")
    return lax.all_to_all(parts, "chan", 0, 0, axis_index_groups=z_groups(n))


def along_y(parts):
    n = lax.axis_size("batch")
    return lax.all_to_all(parts, "batch", 0, 0, axis_index_groups=y_groups(n))


def along_batch(parts):
    return lax.all_to_all(parts, "batch", 0, 0)


def copies(value, n):
    return jnp.broadcast_to(value[None], (n,) + value.shape)


def by_xz(array, n):
    block = array.shape[0] // n
    split = array.reshape(n // NX, NX, block, *array.shape[1:])
    return jnp.swapaxes(split, 0, 1).reshape(array.shape)


def after(value, *others):
    return lax.optimization_barrier((value, *others))[0]


def partner(value, axis, step):
    n = lax.axis_size(axis)
    return lax.ppermute(value, axis, [(i, i ^ step) for i in range(n)])


def dot(a, b, dims=None):
    if dims is None:
        return jnp.dot(a, b, preferred_element_type=F32)
    return lax.dot_general(a, b, dims, preferred_element_type=F32)


def call(kernel, outs, arrays, scratch=(), far_in=(), far_out=()):
    n_in, n_out, n_scratch = len(arrays), len(outs), len(scratch)
    vmem = pl.BlockSpec(memory_space=pltpu.VMEM)
    far = pl.BlockSpec(memory_space=pl.ANY)
    held = [pltpu.VMEM(arrays[k].shape, arrays[k].dtype) for k in far_in]
    held += [pltpu.VMEM(*outs[k]) for k in far_out]
    scratch = list(scratch) + held
    n_far = len(held)
    if n_far:
        scratch.append(pltpu.SemaphoreType.DMA((n_far,)))

    def run(*refs):
        near = list(refs[: n_in + n_out])
        if not n_far:
            kernel(*refs)
            return
        buffers, sems = refs[n_in + n_out + n_scratch : -1], refs[-1]
        moves = []
        for i, k in enumerate(far_in):
            moves.append(pltpu.make_async_copy(refs[k], buffers[i], sems.at[i]))
            near[k] = buffers[i]
        flights = {}
        for i, k in enumerate(far_out, len(far_in)):
            flights[k] = pltpu.make_async_copy(buffers[i], refs[n_in + k], sems.at[i])
            near[n_in + k] = buffers[i]
        for move in moves:
            move.start()
        for move in moves:
            move.wait()
        started = []

        def flush(k):
            flights[k].start()
            started.append(k)

        kernel(*near, *refs[n_in + n_out : n_in + n_out + n_scratch], flush=flush)
        for k in far_out:
            if k not in started:
                flush(k)
        for k in far_out:
            flights[k].wait()

    return pl.pallas_call(
        run,
        out_shape=tuple(jax.ShapeDtypeStruct(shape, dtype) for shape, dtype in outs),
        in_specs=[far if k in far_in else vmem for k in range(n_in)],
        out_specs=tuple(far if k in far_out else vmem for k in range(n_out)),
        scratch_shapes=scratch,
        compiler_params=pltpu.CompilerParams(
            vmem_limit_bytes=FAR_LIMIT if n_far else VMEM_LIMIT
        ),
    )(*arrays)


def lane_of(lanes):
    return lax.broadcasted_iota(jnp.int32, (1, lanes), 1)


def column_tile(first, second, start):
    lane = lane_of(LANES)
    return jnp.where(lane == start, first, jnp.where(lane == start + 1, second, 0.0))


def write_edges(out_ref, value, first, second, columns, me):
    local = value.shape[1]
    lane = lane_of(LANES)
    sums = column_tile(first, second, columns)
    low = jnp.where(lane < columns, value[:, :LANES], sums)
    last = pltpu.roll(value[:, local - LANES :], columns, 1)
    high = jnp.where(lane < columns, last, sums)
    for peer in range(out_ref.shape[0]):
        out_ref[peer] = jnp.where(me > peer, low, high)


def read_edges(in_ref, columns, me):
    count = in_ref.shape[0]
    total = in_ref[0]
    for peer in range(1, count):
        total = total + in_ref[peer]
    beyond = in_ref[jnp.minimum(me + 1, count - 1)]
    before = pltpu.roll(in_ref[jnp.maximum(me - 1, 0)], columns, 1)
    edge = jnp.where(lane_of(LANES) < columns, beyond, before)
    return edge, total[:, columns : columns + 1], total[:, columns + 1 : columns + 2]


def write_rows(out_ref, first, second):
    rows = column_tile(first, second, 0).T[:8]
    for peer in range(out_ref.shape[0]):
        out_ref[peer] = rows


def read_rows(in_ref):
    total = in_ref[0]
    for peer in range(1, in_ref.shape[0]):
        total = total + in_ref[peer]
    square = jnp.concatenate([total, jnp.zeros((LANES - 8, LANES), F32)], 0).T
    return total, square[:, 0:1], square[:, 1:2]


def shifted(value, offset, local):
    if offset != 0:
        value = pltpu.roll(value, (-offset) % value.shape[1], 1)
    return value[:, :local]


def conv_kernel(columns, x_ref, edge_ref, taps_ref, conv_ref, own_ref, pay_ref, part_ref):
    width, local = conv_ref.shape
    channels = x_ref.shape[1]
    part_ref[:, :local] = dot(taps_ref[...], x_ref[...], NT)
    part_ref[:, local:] = dot(taps_ref[...], edge_ref[...], NT)
    row = lax.broadcasted_iota(jnp.int32, (width, channels), 0) + lax.axis_index("chan") * width
    col = lax.broadcasted_iota(jnp.int32, (width, channels), 1)
    own_ref[...] = dot(jnp.where(row == col, 1.0, 0.0).astype(BF16), x_ref[...], NT)
    column = lax.rem(lane_of(local), columns)
    conv = jnp.zeros((width, local), F32)
    for tap in range(9):
        tap_row, tap_col = divmod(tap, 3)
        offset = (tap_row - 1) * columns + tap_col - 1
        piece = shifted(part_ref[tap * width : (tap + 1) * width, :], offset, local)
        if tap_col == 0:
            piece = jnp.where(column > 0, piece, 0.0)
        if tap_col == 2:
            piece = jnp.where(column < columns - 1, piece, 0.0)
        conv = conv + piece
    conv_ref[...] = conv
    first = jnp.sum(conv, 1, keepdims=True)
    second = jnp.sum(conv * conv, 1, keepdims=True)
    write_edges(pay_ref, conv, first, second, columns, lax.axis_index("batch"))


def stream_kernel(
    columns, pixels, conv_ref, own_ref, recv_ref, gain_ref, bias_ref, out_ref, norm_ref, fact_ref
):
    local = conv_ref.shape[1]
    edge, first, second = read_edges(recv_ref, columns, lax.axis_index("batch"))
    mean = first / pixels
    scale = lax.rsqrt(second / pixels - mean * mean + EPSILON)
    norm = (conv_ref[...] - mean) * scale
    norm_ref[:, :local] = norm
    norm_ref[:, local:] = (edge - mean) * scale
    pre = gain_ref[...] * norm + bias_ref[...]
    stream = (own_ref[...] + jnp.maximum(pre, 0.0)).astype(BF16)
    for peer in range(out_ref.shape[0]):
        out_ref[peer] = stream
    fact_ref[...] = jnp.broadcast_to(gain_ref[...] * scale, fact_ref.shape)


def hidden_kernel(full_ref, up_ref, hidden_ref, pay_ref):
    depth = full_ref.shape[1]
    hidden = jnp.zeros(hidden_ref.shape, F32)
    for i in range(NX):
        hidden = hidden + dot(up_ref[:, i * depth : (i + 1) * depth], full_ref[i])
    hidden_ref[...] = hidden
    write_rows(
        pay_ref,
        jnp.sum(hidden, 1, keepdims=True),
        jnp.sum(hidden * hidden, 1, keepdims=True),
    )


def active_kernel(
    pixels, hidden_ref, cotan_ref, recv_ref, gain_ref, bias_ref, cols_ref, rows_ref,
    act_ref, norm_ref, masked_ref, pay_ref, fact_ref, term_ref, flush,
):
    _, first, second = read_rows(recv_ref)
    mean = first / pixels
    scale = lax.rsqrt(second / pixels - mean * mean + EPSILON)
    norm = (hidden_ref[...] - mean) * scale
    pre = gain_ref[...] * norm + bias_ref[...]
    act = jnp.maximum(pre, 0.0).astype(BF16)
    act_ref[...] = act
    flush(0)
    masked = jnp.where(pre > 0, dot(cols_ref[...], cotan_ref[...]), 0.0)
    norm_ref[...] = norm
    flush(1)
    masked_ref[...] = masked
    flush(2)
    fact_ref[...] = jnp.broadcast_to(gain_ref[...] * scale, fact_ref.shape)
    flush(4)
    write_rows(
        pay_ref,
        jnp.sum(masked, 1, keepdims=True),
        jnp.sum(masked * norm, 1, keepdims=True),
    )
    depth = term_ref.shape[0] // NX
    for i in range(NX):
        part = slice(i * depth, (i + 1) * depth)
        term_ref[part] = dot(rows_ref[part], act).astype(BF16)


def term_kernel(
    pixels, masked_ref, norm_ref, recv_ref, fact_ref, up_ref, delta_ref, term_ref, sums_ref
):
    total, first, second = read_rows(recv_ref)
    sums_ref[...] = total
    delta = fact_ref[:, 0:1] * (
        masked_ref[...] - first / pixels - norm_ref[...] * second / pixels
    )
    delta = delta.astype(BF16)
    delta_ref[...] = delta
    depth = term_ref.shape[1]
    for i in range(NX):
        part = slice(i * depth, (i + 1) * depth)
        term_ref[i] = dot(up_ref[part], delta).astype(BF16)


def weight_kernel(full_ref, cotan_ref, delta_ref, act_ref, grad_ref):
    depth = full_ref.shape[1]
    for i in range(NX):
        grad_ref[i] = dot(full_ref[i], delta_ref[...], NT).astype(BF16)
        cotan = cotan_ref[i * depth : (i + 1) * depth]
        grad_ref[NX + i] = dot(cotan, act_ref[...], NT).astype(BF16)


def sum_kernel(recv_ref, *refs):
    out_ref = refs[-1]
    rows = recv_ref.shape[1] // out_ref.shape[0]
    for z in range(out_ref.shape[0]):
        part = slice(z * rows, (z + 1) * rows)
        total = recv_ref[0, part].astype(F32)
        for i in range(1, NX):
            total = total + recv_ref[i, part].astype(F32)
        out_ref[z, :rows] = total.astype(BF16)
        for k, ref in enumerate(refs[:-1]):
            out_ref[z, (k + 1) * rows : (k + 2) * rows] = ref[part]


def grad_kernel(
    columns, recv_ref, cotan_ref, norm_ref, gain_ref, bias_ref, grad_ref, masked_ref, pay_ref
):
    width, local = grad_ref.shape
    total = recv_ref[0].astype(F32)
    for z in range(1, recv_ref.shape[0]):
        total = total + recv_ref[z].astype(F32)
    grad = cotan_ref[...].astype(F32) + total
    grad_ref[...] = grad
    norm = norm_ref[:, :local]
    masked = jnp.where(gain_ref[...] * norm + bias_ref[...] > 0, grad, 0.0)
    masked_ref[...] = masked
    first = jnp.sum(masked, 1, keepdims=True)
    second = jnp.sum(masked * norm, 1, keepdims=True)
    write_edges(pay_ref, masked, first, second, columns, lax.axis_index("batch"))


def back_kernel(
    columns, pixels, masked_ref, recv_ref, norm_ref, fact_ref, taps_ref, x_ref, weight_ref,
    term_ref, mine_ref, theirs_ref, sums_ref, win_ref,
):
    width, local = masked_ref.shape
    me = lax.axis_index("batch")
    edge, first, second = read_edges(recv_ref, columns, me)
    sums_ref[...] = column_tile(first, second, 0)
    masked = jnp.concatenate([masked_ref[...], edge], 1)
    delta = fact_ref[:, 0:1] * (masked - first / pixels - norm_ref[...] * second / pixels)
    lane = lane_of(local + LANES)
    beyond = (lane >= local) & (lane < local + columns)
    before = lane >= local + columns
    high = jnp.where(me == recv_ref.shape[0] - 1, 1, 0)
    low = jnp.where(me == 0, 1, 0)
    outside = jnp.where(beyond, high, jnp.where(before, low, 0))
    delta = jnp.where(outside > 0, 0.0, delta).astype(BF16).astype(F32)
    column = lax.rem(lane_of(local), columns)
    for tap in range(9):
        tap_row, tap_col = divmod(tap, 3)
        offset = (1 - tap_row) * columns + 1 - tap_col
        piece = shifted(delta, offset, local)
        if tap_col == 0:
            piece = jnp.where(column < columns - 1, piece, 0.0)
        if tap_col == 2:
            piece = jnp.where(column > 0, piece, 0.0)
        win_ref[tap * width : (tap + 1) * width, :] = piece.astype(BF16)
    depth = term_ref.shape[1]
    step = NX * width
    for z in range(depth // width):
        block = dot(taps_ref[:, z * step : (z + 1) * step], win_ref[...], TN).astype(BF16)
        for i in range(NX):
            term_ref[i, z * width : (z + 1) * width, :] = block[i * width : (i + 1) * width]
    rows = win_ref.shape[0]
    for ref, half in ((mine_ref, lax.axis_index("section")), (theirs_ref, 1 - lax.axis_index("section"))):
        for j in range(NY):
            chunk = half * NY + j
            start = pl.multiple_of(chunk * LANES, LANES)
            ref[j, :rows] = dot(win_ref[...], x_ref[:, pl.ds(start, LANES)]).astype(BF16)
            ref[j, rows:] = weight_ref[chunk]


def finish_kernel(recv_ref, grad_ref, stream_ref, grad_x_ref, out_ref):
    width = grad_ref.shape[0]
    total = recv_ref[0].astype(F32)
    for z in range(1, recv_ref.shape[0]):
        total = total + recv_ref[z].astype(F32)
    grad_x_ref[...] = (grad_ref[...] + total[:width]).astype(BF16)
    out_ref[...] = (stream_ref[0].astype(F32) + total[width:]).astype(BF16)


def spread_kernel(line_ref, rest_ref, taps_ref, up_ref, down_ref, hold_ref):
    rows = taps_ref.shape[0]
    width = rows // 9
    mine = lax.axis_index("section") == 0
    for chunk in range(2 * NY):
        j = chunk % NY
        a, b = line_ref[j], rest_ref[j]
        if chunk < NY:
            part = jnp.where(mine, a.astype(F32), b.astype(F32))
        else:
            part = jnp.where(mine, b.astype(F32), a.astype(F32))
        taps_ref[:, chunk * LANES : (chunk + 1) * LANES] = part[:rows]
        target = up_ref if chunk < NX else hold_ref
        for z in range((part.shape[0] - rows) // width):
            at = (z * NX + chunk % NX) * width
            target[at : at + width] = part[rows + z * width : rows + (z + 1) * width]
    for block in range(hold_ref.shape[0] // LANES):
        part = slice(block * LANES, (block + 1) * LANES)
        down_ref[:, part] = hold_ref[part].T


def body(activations, kernel_a, gain_a, bias_a, w_up, gain_b, bias_b, w_down, grad_out):
    rows, columns, channels = activations.shape[2:]
    width = kernel_a.shape[3]
    units = w_up.shape[1]
    n_chan = lax.axis_size("chan")
    n_batch = lax.axis_size("batch")
    nz = n_chan // NX
    local = rows * columns
    pixels = local * n_batch
    gain_a, bias_a = gain_a[:, None], bias_a[:, None]
    gain_b, bias_b = gain_b[:, None], bias_b[:, None]

    x_rows = activations.reshape(local, channels)
    taps = kernel_a.transpose(0, 1, 3, 2).reshape(9 * width, channels)
    cotan_own = grad_out[0, 0].transpose(2, 0, 1).reshape(width, local)
    cotan_line = along_z(copies(cotan_own, nz)).reshape(nz * width, local)
    cotan_full = lax.all_gather(
        cotan_line, "chan", axis_index_groups=x_groups(n_chan), tiled=True
    )
    up = [(i, i + 1) for i in range(n_batch - 1)]
    down = [(j, i) for i, j in up]
    before = lax.ppermute(x_rows[local - columns :], "batch", up)
    beyond = lax.ppermute(x_rows[:columns], "batch", down)
    edge = jnp.concatenate([beyond, before], 0)
    up_rows = by_xz(w_up, n_chan)
    down_rows = by_xz(w_down.T, n_chan)
    up_cols, down_cols = up_rows.T, down_rows.T

    conv_a, source, pay = call(
        functools.partial(conv_kernel, columns),
        [((width, local), F32), ((width, local), F32), ((n_batch, width, LANES), F32)],
        (x_rows, edge, taps),
        [pltpu.VMEM((9 * width, local + 2 * columns), F32)],
    )
    recv = along_batch(after(pay, cotan_line, up_cols, down_cols))
    stream, norm_a, fact_a = call(
        functools.partial(stream_kernel, columns, pixels),
        [
            ((nz, width, local), BF16),
            ((width, local + LANES), F32),
            ((width, LANES), F32),
        ],
        (conv_a, source, recv, gain_a, bias_a),
    )
    stream_line = along_z(stream)
    depth = nz * width
    full = along_x(copies(stream_line.reshape(depth, local), NX))
    hidden, pay = call(
        hidden_kernel,
        [((units, local), F32), ((n_batch, 8, LANES), F32)],
        (full, up_cols),
    )
    act, norm_b, masked_b, pay, fact_b, down_term = call(
        functools.partial(active_kernel, pixels),
        [
            ((units, local), BF16),
            ((units, local), F32),
            ((units, local), F32),
            ((n_batch, 8, LANES), F32),
            ((units, LANES), F32),
            ((channels, local), BF16),
        ],
        (hidden, cotan_full, along_batch(pay), gain_b, bias_b, down_cols, down_rows),
        far_in=(0, 1, 5, 6),
        far_out=(0, 1, 2, 4, 5),
    )
    down_part = lax.psum_scatter(
        down_term, "chan", axis_index_groups=x_groups(n_chan), tiled=True
    )
    delta_u, term, sums_b = call(
        functools.partial(term_kernel, pixels),
        [((units, local), BF16), ((NX, depth, local), BF16), ((8, LANES), F32)],
        (masked_b, norm_b, along_batch(pay), fact_b, up_rows),
    )
    (weight_grad,) = call(
        weight_kernel, [((2 * NX, depth, units), BF16)], (full, cotan_full, delta_u, act)
    )
    (part,) = call(
        sum_kernel, [((nz, width, local), BF16)], (along_x(term),)
    )
    part = after(part, weight_grad, down_part)
    grad_y, masked_a, pay = call(
        functools.partial(grad_kernel, columns),
        [
            ((width, local), F32),
            ((width, local), F32),
            ((n_batch, width, LANES), F32),
        ],
        (along_z(part), cotan_own, norm_a, gain_a, bias_a),
    )
    taps_rows = 9 * width
    chunk_rows = taps_rows + depth
    term, mine, theirs, sums_a = call(
        functools.partial(back_kernel, columns, pixels),
        [
            ((NX, depth, local), BF16),
            ((NY, chunk_rows, LANES), BF16),
            ((NY, chunk_rows, LANES), BF16),
            ((width, LANES), F32),
        ],
        (masked_a, along_batch(pay), norm_a, fact_a, taps, x_rows, weight_grad),
        [pltpu.VMEM((taps_rows, local), BF16)],
    )
    recv = along_x(term)
    theirs = partner(theirs, "section", 1)
    vectors = jnp.concatenate([sums_a[:, :2].T, sums_b[:2]], 1)
    vectors = vectors + partner(vectors, "section", 1)
    half = (mine.astype(F32) + theirs.astype(F32)).astype(BF16)
    recv = after(recv, half, vectors)
    half = along_y(after(half, recv))
    half = jnp.sum(half.astype(F32), 0).astype(BF16)
    across = partner(half, "batch", NY)
    (part,) = call(sum_kernel, [((nz, 2 * width, local), BF16)], (recv, down_part))
    recv = along_z(after(part, half))
    grad_x, out_own = call(
        finish_kernel,
        [((width, local), BF16), ((width, local), BF16)],
        (recv, grad_y, stream),
    )
    half = (half.astype(F32) + across.astype(F32)).astype(BF16)
    line = along_y(copies(after(half, recv), NY))
    rest = partner(line, "section", 1)
    kernel_total, up_total, down_total = call(
        spread_kernel,
        [((taps_rows, channels), F32), ((channels, units), F32), ((units, channels), F32)],
        (line, rest),
        [pltpu.VMEM((channels, units), F32)],
    )
    kernel_total = kernel_total.reshape(3, 3, width, channels).transpose(0, 1, 3, 2)

    def placed(own):
        return own.reshape(width, rows, columns).transpose(1, 2, 0)[None, None]

    return (
        placed(out_own),
        placed(grad_x),
        kernel_total,
        vectors[1, :width],
        vectors[0, :width],
        up_total,
        vectors[1, width:],
        vectors[0, width:],
        down_total,
    )


def solution(mesh):
    placed = (
        P("section", None, "batch", None, None),
        P(None, None, None, "chan"),
        P("chan"),
        P("chan"),
        P(None, "chan"),
        P("chan"),
        P("chan"),
        P("chan", None),
        P("section", None, "batch", None, "chan"),
    )
    return jax.shard_map(
        body,
        mesh=mesh,
        in_specs=placed,
        out_specs=(
            P("section", None, "batch", None, "chan"),
            P("section", None, "batch", None, "chan"),
            P(None, None, None, "chan"),
            P("chan"),
            P("chan"),
            P(None, "chan"),
            P("chan"),
            P("chan"),
            P("chan", None),
        ),
        check_vma=False,
    )
```

```python
import functools

import jax
import jax.numpy as jnp
from jax import lax
from jax.experimental import pallas as pl
from jax.experimental.pallas import tpu as pltpu
from jax.sharding import PartitionSpec as P

EPSILON = 1e-05
F32 = jnp.float32
BF16 = jnp.bfloat16
NX = 4
NY = 4
LANES = 128
VMEM_LIMIT = 12 << 20
FAR_LIMIT = 56 << 20
NT = (((1,), (1,)), ((), ()))
TN = (((0,), (0,)), ((), ()))


def x_groups(n):
    return [[NX * z + i for i in range(NX)] for z in range(n // NX)]


def z_groups(n):
    return [[NX * z + i for z in range(n // NX)] for i in range(NX)]


def y_groups(n):
    return [[NY * z + i for i in range(NY)] for z in range(n // NY)]


def along_x(parts):
    n = lax.axis_size("chan")
    return lax.all_to_all(parts, "chan", 0, 0, axis_index_groups=x_groups(n))


def along_z(parts):
    n = lax.axis_size("chan")
    return lax.all_to_all(parts, "chan", 0, 0, axis_index_groups=z_groups(n))


def along_y(parts):
    n = lax.axis_size("batch")
    return lax.all_to_all(parts, "batch", 0, 0, axis_index_groups=y_groups(n))


def along_batch(parts):
    return lax.all_to_all(parts, "batch", 0, 0)


def copies(value, n):
    return jnp.broadcast_to(value[None], (n,) + value.shape)


def by_xz(array, n):
    block = array.shape[0] // n
    split = array.reshape(n // NX, NX, block, *array.shape[1:])
    return jnp.swapaxes(split, 0, 1).reshape(array.shape)


def after(value, *others):
    return lax.optimization_barrier((value, *others))[0]


def partner(value, axis, step):
    n = lax.axis_size(axis)
    return lax.ppermute(value, axis, [(i, i ^ step) for i in range(n)])


def dot(a, b, dims=None):
    if dims is None:
        return jnp.dot(a, b, preferred_element_type=F32)
    return lax.dot_general(a, b, dims, preferred_element_type=F32)


def call(kernel, outs, arrays, scratch=(), far_in=(), far_out=()):
    n_in, n_out, n_scratch = len(arrays), len(outs), len(scratch)
    vmem = pl.BlockSpec(memory_space=pltpu.VMEM)
    far = pl.BlockSpec(memory_space=pl.ANY)
    held = [pltpu.VMEM(arrays[k].shape, arrays[k].dtype) for k in far_in]
    held += [pltpu.VMEM(*outs[k]) for k in far_out]
    scratch = list(scratch) + held
    n_far = len(held)
    if n_far:
        scratch.append(pltpu.SemaphoreType.DMA((n_far,)))

    def run(*refs):
        near = list(refs[: n_in + n_out])
        if not n_far:
            kernel(*refs)
            return
        buffers, sems = refs[n_in + n_out + n_scratch : -1], refs[-1]
        moves = []
        for i, k in enumerate(far_in):
            moves.append(pltpu.make_async_copy(refs[k], buffers[i], sems.at[i]))
            near[k] = buffers[i]
        flights = {}
        for i, k in enumerate(far_out, len(far_in)):
            flights[k] = pltpu.make_async_copy(buffers[i], refs[n_in + k], sems.at[i])
            near[n_in + k] = buffers[i]
        for move in moves:
            move.start()
        for move in moves:
            move.wait()
        started = []

        def flush(k):
            flights[k].start()
            started.append(k)

        kernel(*near, *refs[n_in + n_out : n_in + n_out + n_scratch], flush=flush)
        for k in far_out:
            if k not in started:
                flush(k)
        for k in far_out:
            flights[k].wait()

    return pl.pallas_call(
        run,
        out_shape=tuple(jax.ShapeDtypeStruct(shape, dtype) for shape, dtype in outs),
        in_specs=[far if k in far_in else vmem for k in range(n_in)],
        out_specs=tuple(far if k in far_out else vmem for k in range(n_out)),
        scratch_shapes=scratch,
        compiler_params=pltpu.CompilerParams(
            vmem_limit_bytes=FAR_LIMIT if n_far else VMEM_LIMIT
        ),
    )(*arrays)


def lane_of(lanes):
    return lax.broadcasted_iota(jnp.int32, (1, lanes), 1)


def column_tile(first, second, start):
    lane = lane_of(LANES)
    return jnp.where(lane == start, first, jnp.where(lane == start + 1, second, 0.0))


def square_of(rows):
    pad = jnp.zeros((LANES - rows.shape[0], LANES), F32)
    return jnp.concatenate([rows, pad], 0).T


def write_edges(out_ref, value, first, second, columns, me):
    width, local = value.shape
    half = width // 2
    left = lane_of(LANES) < columns
    sums = square_of(column_tile(first, second, 0))[:8]
    head, last = value[:, :LANES], value[:, local - LANES :]
    low = jnp.where(left, head[:half], pltpu.roll(head[half:], columns, 1))
    high = jnp.where(left, pltpu.roll(last[:half], columns, 1), last[half:])
    for peer in range(out_ref.shape[0]):
        out_ref[peer, :half] = jnp.where(me > peer, low, high)
        out_ref[peer, half:] = sums


def read_edges(in_ref, columns, me):
    count, rows = in_ref.shape[:2]
    half = rows - 8
    total = in_ref[0, half:]
    for peer in range(1, count):
        total = total + in_ref[peer, half:]
    beyond = in_ref[jnp.minimum(me + 1, count - 1)][:half]
    before = in_ref[jnp.maximum(me - 1, 0)][:half]
    left = lane_of(LANES) < columns
    top = jnp.where(left, beyond, pltpu.roll(before, columns, 1))
    low = jnp.where(left, pltpu.roll(beyond, columns, 1), before)
    square = square_of(total)[: 2 * half]
    return jnp.concatenate([top, low], 0), square[:, 0:1], square[:, 1:2]


def write_rows(out_ref, first, second):
    rows = column_tile(first, second, 0).T[:8]
    for peer in range(out_ref.shape[0]):
        out_ref[peer] = rows


def read_rows(in_ref):
    total = in_ref[0]
    for peer in range(1, in_ref.shape[0]):
        total = total + in_ref[peer]
    square = jnp.concatenate([total, jnp.zeros((LANES - 8, LANES), F32)], 0).T
    return total, square[:, 0:1], square[:, 1:2]


def shifted(value, offset, local):
    if offset != 0:
        value = pltpu.roll(value, (-offset) % value.shape[1], 1)
    return value[:, :local]


def conv_kernel(columns, x_ref, edge_ref, taps_ref, conv_ref, own_ref, pay_ref, part_ref):
    width, local = conv_ref.shape
    channels = x_ref.shape[1]
    part_ref[:, :local] = dot(taps_ref[...], x_ref[...], NT)
    part_ref[:, local:] = dot(taps_ref[...], edge_ref[...], NT)
    row = lax.broadcasted_iota(jnp.int32, (width, channels), 0) + lax.axis_index("chan") * width
    col = lax.broadcasted_iota(jnp.int32, (width, channels), 1)
    own_ref[...] = dot(jnp.where(row == col, 1.0, 0.0).astype(BF16), x_ref[...], NT)
    column = lax.rem(lane_of(local), columns)
    conv = jnp.zeros((width, local), F32)
    for tap in range(9):
        tap_row, tap_col = divmod(tap, 3)
        offset = (tap_row - 1) * columns + tap_col - 1
        piece = shifted(part_ref[tap * width : (tap + 1) * width, :], offset, local)
        if tap_col == 0:
            piece = jnp.where(column > 0, piece, 0.0)
        if tap_col == 2:
            piece = jnp.where(column < columns - 1, piece, 0.0)
        conv = conv + piece
    conv_ref[...] = conv
    first = jnp.sum(conv, 1, keepdims=True)
    second = jnp.sum(conv * conv, 1, keepdims=True)
    write_edges(pay_ref, conv, first, second, columns, lax.axis_index("batch"))


def stream_kernel(
    columns, pixels, conv_ref, own_ref, recv_ref, gain_ref, bias_ref, out_ref, norm_ref, fact_ref
):
    local = conv_ref.shape[1]
    edge, first, second = read_edges(recv_ref, columns, lax.axis_index("batch"))
    mean = first / pixels
    scale = lax.rsqrt(second / pixels - mean * mean + EPSILON)
    norm = (conv_ref[...] - mean) * scale
    norm_ref[:, :local] = norm
    norm_ref[:, local:] = (edge - mean) * scale
    pre = gain_ref[...] * norm + bias_ref[...]
    stream = (own_ref[...] + jnp.maximum(pre, 0.0)).astype(BF16)
    for peer in range(out_ref.shape[0]):
        out_ref[peer] = stream
    fact_ref[...] = jnp.broadcast_to(gain_ref[...] * scale, fact_ref.shape)


def hidden_kernel(full_ref, up_ref, hidden_ref, pay_ref):
    depth = full_ref.shape[1]
    hidden = jnp.zeros(hidden_ref.shape, F32)
    for i in range(NX):
        hidden = hidden + dot(up_ref[:, i * depth : (i + 1) * depth], full_ref[i])
    hidden_ref[...] = hidden
    write_rows(
        pay_ref,
        jnp.sum(hidden, 1, keepdims=True),
        jnp.sum(hidden * hidden, 1, keepdims=True),
    )


def active_kernel(
    pixels, hidden_ref, cotan_ref, recv_ref, gain_ref, bias_ref, cols_ref, rows_ref,
    act_ref, norm_ref, masked_ref, pay_ref, fact_ref, term_ref, flush,
):
    _, first, second = read_rows(recv_ref)
    mean = first / pixels
    scale = lax.rsqrt(second / pixels - mean * mean + EPSILON)
    norm = (hidden_ref[...] - mean) * scale
    pre = gain_ref[...] * norm + bias_ref[...]
    act = jnp.maximum(pre, 0.0).astype(BF16)
    act_ref[...] = act
    flush(0)
    masked = jnp.where(pre > 0, dot(cols_ref[...], cotan_ref[...]), 0.0)
    norm_ref[...] = norm
    flush(1)
    masked_ref[...] = masked
    flush(2)
    fact_ref[...] = jnp.broadcast_to(gain_ref[...] * scale, fact_ref.shape)
    flush(4)
    write_rows(
        pay_ref,
        jnp.sum(masked, 1, keepdims=True),
        jnp.sum(masked * norm, 1, keepdims=True),
    )
    depth = term_ref.shape[0] // NX
    for i in range(NX):
        part = slice(i * depth, (i + 1) * depth)
        term_ref[part] = dot(rows_ref[part], act).astype(BF16)


def term_kernel(
    pixels, masked_ref, norm_ref, recv_ref, fact_ref, up_ref, delta_ref, term_ref, sums_ref
):
    total, first, second = read_rows(recv_ref)
    sums_ref[...] = total
    delta = fact_ref[:, 0:1] * (
        masked_ref[...] - first / pixels - norm_ref[...] * second / pixels
    )
    delta = delta.astype(BF16)
    delta_ref[...] = delta
    depth = term_ref.shape[1]
    for i in range(NX):
        part = slice(i * depth, (i + 1) * depth)
        term_ref[i] = dot(up_ref[part], delta).astype(BF16)


def weight_kernel(full_ref, cotan_ref, delta_ref, act_ref, grad_ref):
    depth = full_ref.shape[1]
    for i in range(NX):
        grad_ref[i] = dot(full_ref[i], delta_ref[...], NT).astype(BF16)
        cotan = cotan_ref[i * depth : (i + 1) * depth]
        grad_ref[NX + i] = dot(cotan, act_ref[...], NT).astype(BF16)


def sum_kernel(recv_ref, *refs):
    out_ref = refs[-1]
    rows = recv_ref.shape[1] // out_ref.shape[0]
    for z in range(out_ref.shape[0]):
        part = slice(z * rows, (z + 1) * rows)
        total = recv_ref[0, part].astype(F32)
        for i in range(1, NX):
            total = total + recv_ref[i, part].astype(F32)
        out_ref[z, :rows] = total.astype(BF16)
        for k, ref in enumerate(refs[:-1]):
            out_ref[z, (k + 1) * rows : (k + 2) * rows] = ref[part]


def grad_kernel(
    columns, recv_ref, cotan_ref, norm_ref, gain_ref, bias_ref, grad_ref, masked_ref, pay_ref
):
    width, local = grad_ref.shape
    total = recv_ref[0].astype(F32)
    for z in range(1, recv_ref.shape[0]):
        total = total + recv_ref[z].astype(F32)
    grad = cotan_ref[...].astype(F32) + total
    grad_ref[...] = grad
    norm = norm_ref[:, :local]
    masked = jnp.where(gain_ref[...] * norm + bias_ref[...] > 0, grad, 0.0)
    masked_ref[...] = masked
    first = jnp.sum(masked, 1, keepdims=True)
    second = jnp.sum(masked * norm, 1, keepdims=True)
    write_edges(pay_ref, masked, first, second, columns, lax.axis_index("batch"))


def back_kernel(
    columns, pixels, masked_ref, recv_ref, norm_ref, fact_ref, taps_ref, x_ref, weight_ref,
    term_ref, mine_ref, theirs_ref, sums_ref, win_ref,
):
    width, local = masked_ref.shape
    me = lax.axis_index("batch")
    edge, first, second = read_edges(recv_ref, columns, me)
    sums_ref[...] = column_tile(first, second, 0)
    masked = jnp.concatenate([masked_ref[...], edge], 1)
    delta = fact_ref[:, 0:1] * (masked - first / pixels - norm_ref[...] * second / pixels)
    lane = lane_of(local + LANES)
    beyond = (lane >= local) & (lane < local + columns)
    before = lane >= local + columns
    high = jnp.where(me == recv_ref.shape[0] - 1, 1, 0)
    low = jnp.where(me == 0, 1, 0)
    outside = jnp.where(beyond, high, jnp.where(before, low, 0))
    delta = jnp.where(outside > 0, 0.0, delta).astype(BF16).astype(F32)
    column = lax.rem(lane_of(local), columns)
    for tap in range(9):
        tap_row, tap_col = divmod(tap, 3)
        offset = (1 - tap_row) * columns + 1 - tap_col
        piece = shifted(delta, offset, local)
        if tap_col == 0:
            piece = jnp.where(column < columns - 1, piece, 0.0)
        if tap_col == 2:
            piece = jnp.where(column > 0, piece, 0.0)
        win_ref[tap * width : (tap + 1) * width, :] = piece.astype(BF16)
    depth = term_ref.shape[1]
    step = NX * width
    for z in range(depth // width):
        block = dot(taps_ref[:, z * step : (z + 1) * step], win_ref[...], TN).astype(BF16)
        for i in range(NX):
            term_ref[i, z * width : (z + 1) * width, :] = block[i * width : (i + 1) * width]
    rows = win_ref.shape[0]
    for ref, half in ((mine_ref, lax.axis_index("section")), (theirs_ref, 1 - lax.axis_index("section"))):
        for j in range(NY):
            chunk = half * NY + j
            start = pl.multiple_of(chunk * LANES, LANES)
            ref[j, :rows] = dot(win_ref[...], x_ref[:, pl.ds(start, LANES)]).astype(BF16)
            ref[j, rows:] = weight_ref[chunk]


def finish_kernel(recv_ref, grad_ref, stream_ref, grad_x_ref, out_ref):
    width = grad_ref.shape[0]
    total = recv_ref[0].astype(F32)
    for z in range(1, recv_ref.shape[0]):
        total = total + recv_ref[z].astype(F32)
    grad_x_ref[...] = (grad_ref[...] + total[:width]).astype(BF16)
    out_ref[...] = (stream_ref[0].astype(F32) + total[width:]).astype(BF16)


def spread_kernel(line_ref, rest_ref, taps_ref, up_ref, down_ref, hold_ref):
    rows = taps_ref.shape[0]
    width = rows // 9
    mine = lax.axis_index("section") == 0
    for chunk in range(2 * NY):
        j = chunk % NY
        a, b = line_ref[j], rest_ref[j]
        if chunk < NY:
            part = jnp.where(mine, a.astype(F32), b.astype(F32))
        else:
            part = jnp.where(mine, b.astype(F32), a.astype(F32))
        taps_ref[:, chunk * LANES : (chunk + 1) * LANES] = part[:rows]
        target = up_ref if chunk < NX else hold_ref
        for z in range((part.shape[0] - rows) // width):
            at = (z * NX + chunk % NX) * width
            target[at : at + width] = part[rows + z * width : rows + (z + 1) * width]
    for block in range(hold_ref.shape[0] // LANES):
        part = slice(block * LANES, (block + 1) * LANES)
        down_ref[:, part] = hold_ref[part].T


def body(activations, kernel_a, gain_a, bias_a, w_up, gain_b, bias_b, w_down, grad_out):
    rows, columns, channels = activations.shape[2:]
    width = kernel_a.shape[3]
    units = w_up.shape[1]
    n_chan = lax.axis_size("chan")
    n_batch = lax.axis_size("batch")
    nz = n_chan // NX
    local = rows * columns
    pixels = local * n_batch
    gain_a, bias_a = gain_a[:, None], bias_a[:, None]
    gain_b, bias_b = gain_b[:, None], bias_b[:, None]

    x_rows = activations.reshape(local, channels)
    taps = kernel_a.transpose(0, 1, 3, 2).reshape(9 * width, channels)
    cotan_own = grad_out[0, 0].transpose(2, 0, 1).reshape(width, local)
    cotan_line = along_z(copies(cotan_own, nz)).reshape(nz * width, local)
    cotan_full = lax.all_gather(
        cotan_line, "chan", axis_index_groups=x_groups(n_chan), tiled=True
    )
    up = [(i, i + 1) for i in range(n_batch - 1)]
    down = [(j, i) for i, j in up]
    before = lax.ppermute(x_rows[local - columns :], "batch", up)
    beyond = lax.ppermute(x_rows[:columns], "batch", down)
    edge = jnp.concatenate([beyond, before], 0)
    up_rows = by_xz(w_up, n_chan)
    down_rows = by_xz(w_down.T, n_chan)
    up_cols, down_cols = up_rows.T, down_rows.T

    conv_a, source, pay = call(
        functools.partial(conv_kernel, columns),
        [((width, local), F32), ((width, local), F32), ((n_batch, width // 2 + 8, LANES), F32)],
        (x_rows, edge, taps),
        [pltpu.VMEM((9 * width, local + 2 * columns), F32)],
    )
    recv = along_batch(after(pay, cotan_line, up_cols, down_cols))
    stream, norm_a, fact_a = call(
        functools.partial(stream_kernel, columns, pixels),
        [
            ((nz, width, local), BF16),
            ((width, local + LANES), F32),
            ((width, LANES), F32),
        ],
        (conv_a, source, recv, gain_a, bias_a),
    )
    stream_line = along_z(stream)
    depth = nz * width
    full = along_x(copies(stream_line.reshape(depth, local), NX))
    hidden, pay = call(
        hidden_kernel,
        [((units, local), F32), ((n_batch, 8, LANES), F32)],
        (full, up_cols),
    )
    act, norm_b, masked_b, pay, fact_b, down_term = call(
        functools.partial(active_kernel, pixels),
        [
            ((units, local), BF16),
            ((units, local), F32),
            ((units, local), F32),
            ((n_batch, 8, LANES), F32),
            ((units, LANES), F32),
            ((channels, local), BF16),
        ],
        (hidden, cotan_full, along_batch(pay), gain_b, bias_b, down_cols, down_rows),
        far_in=(0, 1, 5, 6),
        far_out=(0, 1, 2, 4, 5),
    )
    down_part = lax.psum_scatter(
        down_term, "chan", axis_index_groups=x_groups(n_chan), tiled=True
    )
    delta_u, term, sums_b = call(
        functools.partial(term_kernel, pixels),
        [((units, local), BF16), ((NX, depth, local), BF16), ((8, LANES), F32)],
        (masked_b, norm_b, along_batch(pay), fact_b, up_rows),
    )
    (weight_grad,) = call(
        weight_kernel, [((2 * NX, depth, units), BF16)], (full, cotan_full, delta_u, act)
    )
    (part,) = call(
        sum_kernel, [((nz, width, local), BF16)], (along_x(term),)
    )
    part = after(part, weight_grad, down_part)
    grad_y, masked_a, pay = call(
        functools.partial(grad_kernel, columns),
        [
            ((width, local), F32),
            ((width, local), F32),
            ((n_batch, width // 2 + 8, LANES), F32),
        ],
        (along_z(part), cotan_own, norm_a, gain_a, bias_a),
    )
    taps_rows = 9 * width
    chunk_rows = taps_rows + depth
    term, mine, theirs, sums_a = call(
        functools.partial(back_kernel, columns, pixels),
        [
            ((NX, depth, local), BF16),
            ((NY, chunk_rows, LANES), BF16),
            ((NY, chunk_rows, LANES), BF16),
            ((width, LANES), F32),
        ],
        (masked_a, along_batch(pay), norm_a, fact_a, taps, x_rows, weight_grad),
        [pltpu.VMEM((taps_rows, local), BF16)],
    )
    recv = along_x(term)
    theirs = partner(theirs, "section", 1)
    vectors = jnp.concatenate([sums_a[:, :2].T, sums_b[:2]], 1)
    vectors = vectors + partner(vectors, "section", 1)
    half = (mine.astype(F32) + theirs.astype(F32)).astype(BF16)
    recv = after(recv, half, vectors)
    half = along_y(after(half, recv))
    half = jnp.sum(half.astype(F32), 0).astype(BF16)
    across = partner(half, "batch", NY)
    (part,) = call(sum_kernel, [((nz, 2 * width, local), BF16)], (recv, down_part))
    recv = along_z(after(part, half))
    grad_x, out_own = call(
        finish_kernel,
        [((width, local), BF16), ((width, local), BF16)],
        (recv, grad_y, stream),
    )
    half = (half.astype(F32) + across.astype(F32)).astype(BF16)
    line = along_y(copies(after(half, recv), NY))
    rest = partner(line, "section", 1)
    kernel_total, up_total, down_total = call(
        spread_kernel,
        [((taps_rows, channels), F32), ((channels, units), F32), ((units, channels), F32)],
        (line, rest),
        [pltpu.VMEM((channels, units), F32)],
    )
    kernel_total = kernel_total.reshape(3, 3, width, channels).transpose(0, 1, 3, 2)

    def placed(own):
        return own.reshape(width, rows, columns).transpose(1, 2, 0)[None, None]

    return (
        placed(out_own),
        placed(grad_x),
        kernel_total,
        vectors[1, :width],
        vectors[0, :width],
        up_total,
        vectors[1, width:],
        vectors[0, width:],
        down_total,
    )


def solution(mesh):
    placed = (
        P("section", None, "batch", None, None),
        P(None, None, None, "chan"),
        P("chan"),
        P("chan"),
        P(None, "chan"),
        P("chan"),
        P("chan"),
        P("chan", None),
        P("section", None, "batch", None, "chan"),
    )
    return jax.shard_map(
        body,
        mesh=mesh,
        in_specs=placed,
        out_specs=(
            P("section", None, "batch", None, "chan"),
            P("section", None, "batch", None, "chan"),
            P(None, None, None, "chan"),
            P("chan"),
            P("chan"),
            P(None, "chan"),
            P("chan"),
            P("chan"),
            P("chan", None),
        ),
        check_vma=False,
    )
```

```python
import functools

import jax
import jax.numpy as jnp
from jax import lax
from jax.experimental import pallas as pl
from jax.experimental.pallas import tpu as pltpu
from jax.sharding import PartitionSpec as P

EPSILON = 1e-05
F32 = jnp.float32
BF16 = jnp.bfloat16
NX = 4
NY = 4
LANES = 128
VMEM_LIMIT = 12 << 20
FAR_LIMIT = 56 << 20
NT = (((1,), (1,)), ((), ()))
TN = (((0,), (0,)), ((), ()))


def x_groups(n):
    return [[NX * z + i for i in range(NX)] for z in range(n // NX)]


def z_groups(n):
    return [[NX * z + i for z in range(n // NX)] for i in range(NX)]


def y_groups(n):
    return [[NY * z + i for i in range(NY)] for z in range(n // NY)]


def along_x(parts):
    n = lax.axis_size("chan")
    return lax.all_to_all(parts, "chan", 0, 0, axis_index_groups=x_groups(n))


def along_z(parts):
    n = lax.axis_size("chan")
    return lax.all_to_all(parts, "chan", 0, 0, axis_index_groups=z_groups(n))


def along_y(parts):
    n = lax.axis_size("batch")
    return lax.all_to_all(parts, "batch", 0, 0, axis_index_groups=y_groups(n))


def along_batch(parts):
    return lax.all_to_all(parts, "batch", 0, 0)


def copies(value, n):
    return jnp.broadcast_to(value[None], (n,) + value.shape)


def by_xz(array, n):
    block = array.shape[0] // n
    split = array.reshape(n // NX, NX, block, *array.shape[1:])
    return jnp.swapaxes(split, 0, 1).reshape(array.shape)


def after(value, *others):
    return lax.optimization_barrier((value, *others))[0]


def partner(value, axis, step):
    n = lax.axis_size(axis)
    return lax.ppermute(value, axis, [(i, i ^ step) for i in range(n)])


def dot(a, b, dims=None):
    if dims is None:
        return jnp.dot(a, b, preferred_element_type=F32)
    return lax.dot_general(a, b, dims, preferred_element_type=F32)


def call(kernel, outs, arrays, scratch=(), far_in=(), far_out=()):
    n_in, n_out, n_scratch = len(arrays), len(outs), len(scratch)
    vmem = pl.BlockSpec(memory_space=pltpu.VMEM)
    far = pl.BlockSpec(memory_space=pl.ANY)
    held = [pltpu.VMEM(arrays[k].shape, arrays[k].dtype) for k in far_in]
    held += [pltpu.VMEM(*outs[k]) for k in far_out]
    scratch = list(scratch) + held
    n_far = len(held)
    if n_far:
        scratch.append(pltpu.SemaphoreType.DMA((n_far,)))

    def run(*refs):
        near = list(refs[: n_in + n_out])
        if not n_far:
            kernel(*refs)
            return
        buffers, sems = refs[n_in + n_out + n_scratch : -1], refs[-1]
        moves = []
        for i, k in enumerate(far_in):
            moves.append(pltpu.make_async_copy(refs[k], buffers[i], sems.at[i]))
            near[k] = buffers[i]
        flights = {}
        for i, k in enumerate(far_out, len(far_in)):
            flights[k] = pltpu.make_async_copy(buffers[i], refs[n_in + k], sems.at[i])
            near[n_in + k] = buffers[i]
        for move in moves:
            move.start()
        for move in moves:
            move.wait()
        started = []

        def flush(k):
            flights[k].start()
            started.append(k)

        kernel(*near, *refs[n_in + n_out : n_in + n_out + n_scratch], flush=flush)
        for k in far_out:
            if k not in started:
                flush(k)
        for k in far_out:
            flights[k].wait()

    return pl.pallas_call(
        run,
        out_shape=tuple(jax.ShapeDtypeStruct(shape, dtype) for shape, dtype in outs),
        in_specs=[far if k in far_in else vmem for k in range(n_in)],
        out_specs=tuple(far if k in far_out else vmem for k in range(n_out)),
        scratch_shapes=scratch,
        compiler_params=pltpu.CompilerParams(
            vmem_limit_bytes=FAR_LIMIT if n_far else VMEM_LIMIT
        ),
    )(*arrays)


def lane_of(lanes):
    return lax.broadcasted_iota(jnp.int32, (1, lanes), 1)


def column_tile(first, second, start):
    lane = lane_of(LANES)
    return jnp.where(lane == start, first, jnp.where(lane == start + 1, second, 0.0))


def write_edges(out_ref, value, first, second, columns, me):
    local = value.shape[1]
    lane = lane_of(LANES)
    sums = column_tile(first, second, columns)
    low = jnp.where(lane < columns, value[:, :LANES], sums)
    last = pltpu.roll(value[:, local - LANES :], columns, 1)
    high = jnp.where(lane < columns, last, sums)
    for peer in range(out_ref.shape[0]):
        out_ref[peer] = jnp.where(me > peer, low, high)


def read_edges(in_ref, columns, me):
    count = in_ref.shape[0]
    total = in_ref[0]
    for peer in range(1, count):
        total = total + in_ref[peer]
    beyond = in_ref[jnp.minimum(me + 1, count - 1)]
    before = pltpu.roll(in_ref[jnp.maximum(me - 1, 0)], columns, 1)
    edge = jnp.where(lane_of(LANES) < columns, beyond, before)
    return edge, total[:, columns : columns + 1], total[:, columns + 1 : columns + 2]


def write_rows(out_ref, first, second):
    rows = column_tile(first, second, 0).T[:8]
    for peer in range(out_ref.shape[0]):
        out_ref[peer] = rows


def read_rows(in_ref):
    total = in_ref[0]
    for peer in range(1, in_ref.shape[0]):
        total = total + in_ref[peer]
    square = jnp.concatenate([total, jnp.zeros((LANES - 8, LANES), F32)], 0).T
    return total, square[:, 0:1], square[:, 1:2]


def shifted(value, offset, local):
    if offset != 0:
        value = pltpu.roll(value, (-offset) % value.shape[1], 1)
    return value[:, :local]


def conv_kernel(columns, x_ref, edge_ref, taps_ref, conv_ref, own_ref, pay_ref, part_ref):
    width, local = conv_ref.shape
    channels = x_ref.shape[1]
    part_ref[:, :local] = dot(taps_ref[...], x_ref[...], NT)
    part_ref[:, local:] = dot(taps_ref[...], edge_ref[...], NT)
    row = lax.broadcasted_iota(jnp.int32, (width, channels), 0) + lax.axis_index("chan") * width
    col = lax.broadcasted_iota(jnp.int32, (width, channels), 1)
    own_ref[...] = dot(jnp.where(row == col, 1.0, 0.0).astype(BF16), x_ref[...], NT)
    column = lax.rem(lane_of(local), columns)
    conv = jnp.zeros((width, local), F32)
    for tap in range(9):
        tap_row, tap_col = divmod(tap, 3)
        offset = (tap_row - 1) * columns + tap_col - 1
        piece = shifted(part_ref[tap * width : (tap + 1) * width, :], offset, local)
        if tap_col == 0:
            piece = jnp.where(column > 0, piece, 0.0)
        if tap_col == 2:
            piece = jnp.where(column < columns - 1, piece, 0.0)
        conv = conv + piece
    conv_ref[...] = conv
    first = jnp.sum(conv, 1, keepdims=True)
    second = jnp.sum(conv * conv, 1, keepdims=True)
    write_edges(pay_ref, conv, first, second, columns, lax.axis_index("batch"))


def stream_kernel(
    columns, pixels, conv_ref, own_ref, recv_ref, gain_ref, bias_ref, out_ref, norm_ref, fact_ref
):
    local = conv_ref.shape[1]
    edge, first, second = read_edges(recv_ref, columns, lax.axis_index("batch"))
    mean = first / pixels
    scale = lax.rsqrt(second / pixels - mean * mean + EPSILON)
    norm = (conv_ref[...] - mean) * scale
    norm_ref[:, :local] = norm
    norm_ref[:, local:] = (edge - mean) * scale
    pre = gain_ref[...] * norm + bias_ref[...]
    stream = (own_ref[...] + jnp.maximum(pre, 0.0)).astype(BF16)
    for peer in range(out_ref.shape[0]):
        out_ref[peer] = stream
    fact_ref[...] = jnp.broadcast_to(gain_ref[...] * scale, fact_ref.shape)


def hidden_kernel(full_ref, up_ref, hidden_ref, pay_ref):
    depth = full_ref.shape[1]
    hidden = jnp.zeros(hidden_ref.shape, F32)
    for i in range(NX):
        hidden = hidden + dot(up_ref[:, i * depth : (i + 1) * depth], full_ref[i])
    hidden_ref[...] = hidden
    write_rows(
        pay_ref,
        jnp.sum(hidden, 1, keepdims=True),
        jnp.sum(hidden * hidden, 1, keepdims=True),
    )


def active_kernel(
    pixels, hidden_ref, cotan_ref, recv_ref, gain_ref, bias_ref, cols_ref, rows_ref,
    act_ref, norm_ref, masked_ref, pay_ref, fact_ref, term_ref, flush,
):
    _, first, second = read_rows(recv_ref)
    mean = first / pixels
    scale = lax.rsqrt(second / pixels - mean * mean + EPSILON)
    norm = (hidden_ref[...] - mean) * scale
    pre = gain_ref[...] * norm + bias_ref[...]
    act = jnp.maximum(pre, 0.0).astype(BF16)
    act_ref[...] = act
    flush(0)
    masked = jnp.where(pre > 0, dot(cols_ref[...], cotan_ref[...]), 0.0)
    norm_ref[...] = norm
    flush(1)
    masked_ref[...] = masked
    flush(2)
    fact_ref[...] = jnp.broadcast_to(gain_ref[...] * scale, fact_ref.shape)
    flush(4)
    write_rows(
        pay_ref,
        jnp.sum(masked, 1, keepdims=True),
        jnp.sum(masked * norm, 1, keepdims=True),
    )
    depth = term_ref.shape[0] // NX
    for i in range(NX):
        part = slice(i * depth, (i + 1) * depth)
        term_ref[part] = dot(rows_ref[part], act).astype(BF16)


def term_kernel(
    pixels, masked_ref, norm_ref, recv_ref, fact_ref, up_ref, delta_ref, term_ref, sums_ref
):
    total, first, second = read_rows(recv_ref)
    sums_ref[...] = total
    delta = fact_ref[:, 0:1] * (
        masked_ref[...] - first / pixels - norm_ref[...] * second / pixels
    )
    delta = delta.astype(BF16)
    delta_ref[...] = delta
    depth = term_ref.shape[1]
    for i in range(NX):
        part = slice(i * depth, (i + 1) * depth)
        term_ref[i] = dot(up_ref[part], delta).astype(BF16)


def weight_kernel(full_ref, cotan_ref, delta_ref, act_ref, grad_ref):
    depth = full_ref.shape[1]
    for i in range(NX):
        grad_ref[i] = dot(full_ref[i], delta_ref[...], NT).astype(BF16)
        cotan = cotan_ref[i * depth : (i + 1) * depth]
        grad_ref[NX + i] = dot(cotan, act_ref[...], NT).astype(BF16)


def sum_kernel(recv_ref, *refs):
    out_ref = refs[-1]
    rows = recv_ref.shape[1] // out_ref.shape[0]
    for z in range(out_ref.shape[0]):
        part = slice(z * rows, (z + 1) * rows)
        total = recv_ref[0, part].astype(F32)
        for i in range(1, NX):
            total = total + recv_ref[i, part].astype(F32)
        out_ref[z, :rows] = total.astype(BF16)
        for k, ref in enumerate(refs[:-1]):
            out_ref[z, (k + 1) * rows : (k + 2) * rows] = ref[part]


def grad_kernel(
    columns, recv_ref, cotan_ref, norm_ref, gain_ref, bias_ref, grad_ref, masked_ref, pay_ref
):
    width, local = grad_ref.shape
    total = recv_ref[0].astype(F32)
    for z in range(1, recv_ref.shape[0]):
        total = total + recv_ref[z].astype(F32)
    grad = cotan_ref[...].astype(F32) + total
    grad_ref[...] = grad
    norm = norm_ref[:, :local]
    masked = jnp.where(gain_ref[...] * norm + bias_ref[...] > 0, grad, 0.0)
    masked_ref[...] = masked
    first = jnp.sum(masked, 1, keepdims=True)
    second = jnp.sum(masked * norm, 1, keepdims=True)
    write_edges(pay_ref, masked, first, second, columns, lax.axis_index("batch"))


def back_kernel(
    columns, pixels, masked_ref, recv_ref, norm_ref, fact_ref, taps_ref, x_ref, weight_ref,
    term_ref, mine_ref, theirs_ref, sums_ref, win_ref,
):
    width, local = masked_ref.shape
    me = lax.axis_index("batch")
    edge, first, second = read_edges(recv_ref, columns, me)
    sums_ref[...] = column_tile(first, second, 0)
    masked = jnp.concatenate([masked_ref[...], edge], 1)
    delta = fact_ref[:, 0:1] * (masked - first / pixels - norm_ref[...] * second / pixels)
    lane = lane_of(local + LANES)
    beyond = (lane >= local) & (lane < local + columns)
    before = lane >= local + columns
    high = jnp.where(me == recv_ref.shape[0] - 1, 1, 0)
    low = jnp.where(me == 0, 1, 0)
    outside = jnp.where(beyond, high, jnp.where(before, low, 0))
    delta = jnp.where(outside > 0, 0.0, delta).astype(BF16).astype(F32)
    column = lax.rem(lane_of(local), columns)
    for tap in range(9):
        tap_row, tap_col = divmod(tap, 3)
        offset = (1 - tap_row) * columns + 1 - tap_col
        piece = shifted(delta, offset, local)
        if tap_col == 0:
            piece = jnp.where(column < columns - 1, piece, 0.0)
        if tap_col == 2:
            piece = jnp.where(column > 0, piece, 0.0)
        win_ref[tap * width : (tap + 1) * width, :] = piece.astype(BF16)
    depth = term_ref.shape[1]
    step = NX * width
    for z in range(depth // width):
        block = dot(taps_ref[:, z * step : (z + 1) * step], win_ref[...], TN).astype(BF16)
        for i in range(NX):
            term_ref[i, z * width : (z + 1) * width, :] = block[i * width : (i + 1) * width]
    rows = win_ref.shape[0]
    for ref, half in ((mine_ref, lax.axis_index("section")), (theirs_ref, 1 - lax.axis_index("section"))):
        for j in range(NY):
            chunk = half * NY + j
            start = pl.multiple_of(chunk * LANES, LANES)
            ref[j, :rows] = dot(win_ref[...], x_ref[:, pl.ds(start, LANES)]).astype(BF16)
            ref[j, rows:] = weight_ref[chunk]


def finish_kernel(recv_ref, grad_ref, stream_ref, grad_x_ref, out_ref):
    width = grad_ref.shape[0]
    total = recv_ref[0].astype(F32)
    for z in range(1, recv_ref.shape[0]):
        total = total + recv_ref[z].astype(F32)
    grad_x_ref[...] = (grad_ref[...] + total[:width]).astype(BF16)
    out_ref[...] = (stream_ref[0].astype(F32) + total[width:]).astype(BF16)


def spread_kernel(line_ref, rest_ref, taps_ref, up_ref, down_ref, hold_ref):
    rows = taps_ref.shape[0]
    width = rows // 9
    mine = lax.axis_index("section") == 0
    for chunk in range(2 * NY):
        j = chunk % NY
        a, b = line_ref[j], rest_ref[j]
        if chunk < NY:
            part = jnp.where(mine, a.astype(F32), b.astype(F32))
        else:
            part = jnp.where(mine, b.astype(F32), a.astype(F32))
        taps_ref[:, chunk * LANES : (chunk + 1) * LANES] = part[:rows]
        target = up_ref if chunk < NX else hold_ref
        for z in range((part.shape[0] - rows) // width):
            at = (z * NX + chunk % NX) * width
            target[at : at + width] = part[rows + z * width : rows + (z + 1) * width]
    for block in range(hold_ref.shape[0] // LANES):
        part = slice(block * LANES, (block + 1) * LANES)
        down_ref[:, part] = hold_ref[part].T


def body(activations, kernel_a, gain_a, bias_a, w_up, gain_b, bias_b, w_down, grad_out):
    rows, columns, channels = activations.shape[2:]
    width = kernel_a.shape[3]
    units = w_up.shape[1]
    n_chan = lax.axis_size("chan")
    n_batch = lax.axis_size("batch")
    nz = n_chan // NX
    local = rows * columns
    pixels = local * n_batch
    gain_a, bias_a = gain_a[:, None], bias_a[:, None]
    gain_b, bias_b = gain_b[:, None], bias_b[:, None]

    x_rows = activations.reshape(local, channels)
    taps = kernel_a.transpose(0, 1, 3, 2).reshape(9 * width, channels)
    cotan_own = grad_out[0, 0].transpose(2, 0, 1).reshape(width, local)
    cotan_line = along_z(copies(cotan_own, nz)).reshape(nz * width, local)
    cotan_full = lax.all_gather(
        cotan_line, "chan", axis_index_groups=x_groups(n_chan), tiled=True
    )
    up = [(i, i + 1) for i in range(n_batch - 1)]
    down = [(j, i) for i, j in up]
    before = lax.ppermute(x_rows[local - columns :], "batch", up)
    beyond = lax.ppermute(x_rows[:columns], "batch", down)
    edge = jnp.concatenate([beyond, before], 0)
    up_rows = by_xz(w_up, n_chan)
    down_rows = by_xz(w_down.T, n_chan)
    up_cols, down_cols = up_rows.T, down_rows.T

    conv_a, source, pay = call(
        functools.partial(conv_kernel, columns),
        [((width, local), F32), ((width, local), F32), ((n_batch, width, LANES), F32)],
        (x_rows, edge, taps),
        [pltpu.VMEM((9 * width, local + 2 * columns), F32)],
    )
    recv = along_batch(after(pay, cotan_line))
    stream, norm_a, fact_a = call(
        functools.partial(stream_kernel, columns, pixels),
        [
            ((nz, width, local), BF16),
            ((width, local + LANES), F32),
            ((width, LANES), F32),
        ],
        (conv_a, source, recv, gain_a, bias_a),
    )
    stream_line = along_z(stream)
    depth = nz * width
    full = along_x(copies(stream_line.reshape(depth, local), NX))
    hidden, pay = call(
        hidden_kernel,
        [((units, local), F32), ((n_batch, 8, LANES), F32)],
        (full, up_cols),
    )
    act, norm_b, masked_b, pay, fact_b, down_term = call(
        functools.partial(active_kernel, pixels),
        [
            ((units, local), BF16),
            ((units, local), F32),
            ((units, local), F32),
            ((n_batch, 8, LANES), F32),
            ((units, LANES), F32),
            ((channels, local), BF16),
        ],
        (hidden, cotan_full, along_batch(pay), gain_b, bias_b, down_cols, down_rows),
        far_in=(0, 1, 5, 6),
        far_out=(0, 1, 2, 4, 5),
    )
    down_part = lax.psum_scatter(
        down_term, "chan", axis_index_groups=x_groups(n_chan), tiled=True
    )
    delta_u, term, sums_b = call(
        functools.partial(term_kernel, pixels),
        [((units, local), BF16), ((NX, depth, local), BF16), ((8, LANES), F32)],
        (masked_b, norm_b, along_batch(pay), fact_b, up_rows),
    )
    (weight_grad,) = call(
        weight_kernel, [((2 * NX, depth, units), BF16)], (full, cotan_full, delta_u, act)
    )
    (part,) = call(
        sum_kernel, [((nz, width, local), BF16)], (along_x(term),)
    )
    part = after(part, weight_grad, down_part)
    grad_y, masked_a, pay = call(
        functools.partial(grad_kernel, columns),
        [
            ((width, local), F32),
            ((width, local), F32),
            ((n_batch, width, LANES), F32),
        ],
        (along_z(part), cotan_own, norm_a, gain_a, bias_a),
    )
    taps_rows = 9 * width
    chunk_rows = taps_rows + depth
    term, mine, theirs, sums_a = call(
        functools.partial(back_kernel, columns, pixels),
        [
            ((NX, depth, local), BF16),
            ((NY, chunk_rows, LANES), BF16),
            ((NY, chunk_rows, LANES), BF16),
            ((width, LANES), F32),
        ],
        (masked_a, along_batch(pay), norm_a, fact_a, taps, x_rows, weight_grad),
        [pltpu.VMEM((taps_rows, local), BF16)],
    )
    recv = along_x(term)
    theirs = partner(theirs, "section", 1)
    vectors = jnp.concatenate([sums_a[:, :2].T, sums_b[:2]], 1)
    vectors = vectors + partner(vectors, "section", 1)
    half = (mine.astype(F32) + theirs.astype(F32)).astype(BF16)
    recv = after(recv, half, vectors)
    half = along_y(after(half, recv))
    half = jnp.sum(half.astype(F32), 0).astype(BF16)
    across = partner(half, "batch", NY)
    (part,) = call(sum_kernel, [((nz, 2 * width, local), BF16)], (recv, down_part))
    recv = along_z(after(part, half))
    grad_x, out_own = call(
        finish_kernel,
        [((width, local), BF16), ((width, local), BF16)],
        (recv, grad_y, stream),
    )
    half = (half.astype(F32) + across.astype(F32)).astype(BF16)
    line = along_y(copies(after(half, recv), NY))
    rest = partner(line, "section", 1)
    kernel_total, up_total, down_total = call(
        spread_kernel,
        [((taps_rows, channels), F32), ((channels, units), F32), ((units, channels), F32)],
        (line, rest),
        [pltpu.VMEM((channels, units), F32)],
    )
    kernel_total = kernel_total.reshape(3, 3, width, channels).transpose(0, 1, 3, 2)

    def placed(own):
        return own.reshape(width, rows, columns).transpose(1, 2, 0)[None, None]

    return (
        placed(out_own),
        placed(grad_x),
        kernel_total,
        vectors[1, :width],
        vectors[0, :width],
        up_total,
        vectors[1, width:],
        vectors[0, width:],
        down_total,
    )


def solution(mesh):
    placed = (
        P("section", None, "batch", None, None),
        P(None, None, None, "chan"),
        P("chan"),
        P("chan"),
        P(None, "chan"),
        P("chan"),
        P("chan"),
        P("chan", None),
        P("section", None, "batch", None, "chan"),
    )
    return jax.shard_map(
        body,
        mesh=mesh,
        in_specs=placed,
        out_specs=(
            P("section", None, "batch", None, "chan"),
            P("section", None, "batch", None, "chan"),
            P(None, None, None, "chan"),
            P("chan"),
            P("chan"),
            P(None, "chan"),
            P("chan"),
            P("chan"),
            P("chan", None),
        ),
        check_vma=False,
    )
```
